32 devices in a mesh: dp: 8 (over z, x), tensor: 4 (over y, core).
Axes of the slice: x: 2, y: 2, z: 4, core: 2. Of those that a mesh axis runs over, the one named last changes fastest.
Arguments:
- hidden_in: bfloat16 [8192, 2048], P('dp', 'tensor'), may hold values from -6 to 6
- norm1_gain: bfloat16 [2048], replicated, may hold values from 0.5 to 1.5
- w_query: bfloat16 [2048, 2048], P(None, 'tensor'), may hold values from -0.125 to 0.125
- w_key: bfloat16 [2048, 2048], P(None, 'tensor'), may hold values from -0.125 to 0.125
- w_value: bfloat16 [2048, 2048], P(None, 'tensor'), may hold values from -0.125 to 0.125
- w_out: bfloat16 [2048, 2048], P('tensor'), may hold values from -1 to 1
- norm2_gain: bfloat16 [2048], replicated, may hold values from 0.5 to 1.5
- w_gate: bfloat16 [2048, 8192], P(None, 'tensor'), may hold values from -0.125 to 0.125
- w_up: bfloat16 [2048, 8192], P(None, 'tensor'), may hold values from -0.125 to 0.125
- w_down: bfloat16 [8192, 2048], P('tensor'), may hold values from -0.125 to 0.125
- tile_len: int32 [64], P('dp'), may hold values from 0 to 128, as said below
- tile_offset: int32 [64], P('dp'), may hold values from 0 to 7, as said below
- cotangent: bfloat16 [8192, 2048], P('dp', 'tensor'), may hold values from -6 to 6
Outputs:
- layer_out: bfloat16 [8192, 2048], P('dp', 'tensor')
- input_grad: bfloat16 [8192, 2048], P('dp', 'tensor')
- norm1_gain_grad: float32 [2048], P('dp')
- w_query_grad: float32 [2048, 2048], P('dp', 'tensor')
- w_key_grad: float32 [2048, 2048], P('dp', 'tensor')
- w_value_grad: float32 [2048, 2048], P('dp', 'tensor')
- w_out_grad: float32 [2048, 2048], P('tensor', 'dp')
- norm2_gain_grad: float32 [2048], P('dp')
- w_gate_grad: float32 [2048, 8192], P('dp', 'tensor')
- w_up_grad: float32 [2048, 8192], P('dp', 'tensor')
- w_down_grad: float32 [8192, 2048], P('tensor', 'dp')
The draws below stay inside these ranges and needn't reach their ends.
Inputs may be any that keep to these rules, and one draw needn't show every extreme that they name: `tile_len`: each slot block of 8 tiles holds whole sequences in order, each beginning at a tile with offset 0; a tile with offset k > 0 continues the sequence of the tile before it, which then holds 128 tokens; a tile's tokens fill its first rows; tiles without tokens come last in a block and have offset 0; some block holds a sequence of 1024 tokens. `tile_offset`: A sequence spans at most 8 tiles.
All inputs are finite; a program needn't handle non-finite values.
Results may differ from the reference program's by a relative error of at most 0.015.
Values may be sent and summed in bfloat16 or wider, within the bound.
A program may use at most 320 MiB of HBM per device.

```python
from functools import partial
import jax
import jax.numpy as jnp
from jax import lax

D = 2048
H = 32
HD = 64
FF = 8192
TILE = 128
SEQ_TILES = 8
TILES_DEV = 8
CAP = 1024
TOKENS = 8192
N_DP = 8


def tile_layout(key):
    key_parts = jax.random.split(key, 4)
    column = jnp.arange(TILES_DEV, dtype=jnp.int32)[None, :]
    boundary = column % SEQ_TILES == 0
    new_seq = (jax.random.randint(key_parts[0], (N_DP, TILES_DEV), 0, 3) == 0) | boundary
    used_tiles = jax.random.randint(key_parts[1], (N_DP, 1), TILES_DEV // 2, TILES_DEV + 1)
    chosen = jnp.arange(N_DP, dtype=jnp.int32)[:, None] == jax.random.randint(key_parts[2], (), 0, N_DP)
    new_seq = jnp.where(chosen, boundary, new_seq)
    used_tiles = jnp.where(chosen, TILES_DEV, used_tiles)
    live_tile = column < used_tiles
    following = jnp.concatenate([new_seq[:, 1:] | jnp.logical_not(live_tile[:, 1:]), jnp.ones((N_DP, 1), dtype=bool)], axis=1)
    tail_len = jnp.where(chosen, TILE, jax.random.randint(key_parts[3], (N_DP, TILES_DEV), 1, TILE + 1))
    lengths = jnp.where(live_tile, jnp.where(following, tail_len, TILE), 0)
    seq_first = lax.cummax(jnp.where(new_seq, column, 0), axis=1)
    offsets = jnp.where(live_tile, column - seq_first, 0)
    return (lengths.reshape(-1).astype(jnp.int32), offsets.reshape(-1).astype(jnp.int32))


def draw_tile_len(key, part):
    return tile_layout(key)[0]


def draw_tile_offset(key, part):
    return tile_layout(key)[1]


def strengthened(values, own_key, source, target, shards_of, factor):
    def block_of(axis_at):
        return (jnp.arange(values.shape[axis_at]) // (values.shape[axis_at] // shards_of)).reshape((-1,) + (1,) * (values.ndim - 1 - axis_at))

    one_side = jax.random.permutation(own_key, shards_of)[block_of(target)]
    second = (block_of(target) + shards_of // 2) % shards_of
    return jnp.where((block_of(source) == one_side) | (block_of(source) == second), factor * values, values)


def shard_levels(stream_key, shape, cuts, smallest, top_value):
    def one(dim, shards_of):
        heights = jax.random.uniform(jax.random.fold_in(jax.random.fold_in(stream_key, 6), dim), (shards_of,), jnp.float32, smallest / len(cuts), top_value / len(cuts))
        return jnp.repeat(jnp.exp(heights), shape[dim] // shards_of).reshape((-1,) + (1,) * (len(shape) - dim - 1))

    level = one(*cuts[0])
    for cut in cuts[1:]:
        level = level * one(*cut)
    return level


def scatter_about(own_key, extent, scale, reach, pieces=(), kind=jnp.bfloat16):
    loudness = shard_levels(own_key, extent, pieces, -0.22, 0.18) if pieces else 1.0
    entries = jax.random.normal(own_key, extent, jnp.float32) * scale * loudness
    return jnp.minimum(jnp.maximum(entries, -reach), reach).astype(kind)


def bell_draw_with(own_key, shape, spread, most, cuts, heavy, held_as=jnp.bfloat16):
    drawn = spread * jax.random.normal(own_key, shape, jnp.float32)
    if cuts:
        drawn = drawn * shard_levels(own_key, shape, cuts, -0.22, 0.18)
    return jnp.clip(strengthened(drawn, jax.random.fold_in(own_key, 3), *heavy), -most, most).astype(held_as)


def setup_inputs(seed: int = 0) -> dict:
    streams_of = jax.random.split(jax.random.key(seed), 14)
    hidden_in = scatter_about(streams_of[0], (TOKENS, D), 1.0, 6.0, ((0, 8), (1, 4)))
    norm1_gain = jnp.clip(1.0 + 0.1 * jax.random.normal(streams_of[1], (D,), jnp.float32), 0.5, 1.5).astype(jnp.bfloat16)
    w_query = scatter_about(streams_of[2], (D, H * HD), D ** -0.5, 0.125, ((1, 4),))
    w_key = scatter_about(streams_of[3], (D, H * HD), D ** -0.5, 0.125, ((1, 4),))
    w_value = scatter_about(streams_of[4], (D, H * HD), D ** -0.5, 0.125, ((1, 4),))
    w_out = scatter_about(streams_of[5], (H * HD, D), (H * HD // 64) ** -0.5, 1.0, ((0, 4),))
    norm2_gain = jnp.clip(1.0 + 0.1 * jax.random.normal(streams_of[6], (D,), jnp.float32), 0.5, 1.5).astype(jnp.bfloat16)
    w_gate = scatter_about(streams_of[7], (D, FF), D ** -0.5, 0.125, ((1, 4),))
    w_up = scatter_about(streams_of[8], (D, FF), D ** -0.5, 0.125, ((1, 4),))
    w_down = scatter_about(streams_of[9], (FF, D), (FF // 4) ** -0.5, 0.125, ((0, 4),))
    tile_len = draw_tile_len(jax.random.fold_in(streams_of[13], 71), 0)
    tile_offset = draw_tile_offset(jax.random.fold_in(streams_of[13], 71), 0)
    cotangent = bell_draw_with(streams_of[12], (TOKENS, D), 1.0, 6.0, ((0, 8), (1, 4)), (0, 1, 8, 2.0))
    return {"hidden_in": hidden_in, "norm1_gain": norm1_gain, "w_query": w_query, "w_key": w_key, "w_value": w_value, "w_out": w_out, "norm2_gain": norm2_gain, "w_gate": w_gate, "w_up": w_up, "w_down": w_down, "tile_len": tile_len, "tile_offset": tile_offset, "cotangent": cotangent}


@jax.custom_vjp
def low(v):
    return lax.optimization_barrier(v.astype(jnp.bfloat16)).astype(jnp.float32)

@jax.custom_vjp
def low_back(v):
    return v

def low_keep(v):
    return (low(v), None)

def low_pass(kept, grad):
    return (grad,)

def back_keep(v):
    return (v, None)

def back_low(kept, grad):
    return (low(grad),)
low.defvjp(low_keep, low_pass)
low_back.defvjp(back_keep, back_low)

def matmul_high(operand, weight):
    return jnp.dot(operand, weight, precision=lax.Precision.HIGHEST)

def rms_scale(values):
    return lax.rsqrt(lax.optimization_barrier(jnp.mean(values * values, axis=1, keepdims=True)) + 1e-05)

def rotate(values, cosine_tab, sine_tab):
    half_width = values.shape[-1] // 2
    lower_half = values[..., :half_width]
    upper_half = values[..., half_width:]
    return jnp.concatenate([lower_half * cosine_tab - upper_half * sine_tab, upper_half * cosine_tab + lower_half * sine_tab], axis=-1)

def rope_tables(position):
    frequency = jnp.power(130000.0, -2.0 * jnp.arange(HD // 2, dtype=jnp.float32) / HD)
    angles = position[:, None] * frequency[None, :]
    return (jnp.cos(angles)[:, None, :], jnp.sin(angles)[:, None, :])

def row_layout(tile_len, tile_offset):
    tile_count = tile_len.shape[0]
    within = jnp.tile(jnp.arange(TILE, dtype=jnp.int32), tile_count)
    lengths = jnp.repeat(tile_len, TILE)
    starts = jnp.repeat(tile_offset, TILE)
    sequence = jnp.repeat(jnp.cumsum((tile_offset == 0).astype(jnp.int32)), TILE)
    live_rows = (within < lengths).astype(jnp.float32)
    position = (starts * TILE + within).astype(jnp.float32)
    slot_ids = jnp.arange(tile_count * TILE, dtype=jnp.int32)
    allowed = (sequence[:, None] == sequence[None, :]) & (slot_ids[None, :] <= slot_ids[:, None]) & (live_rows[None, :] > 0) | (slot_ids[:, None] == slot_ids[None, :])
    return (live_rows[:, None], position, allowed)

def device_block(weights, dev_block):
    row_vals, lens_block, offs_block = dev_block
    gain_one, w_query, w_key, w_value, w_out, gain_two, w_gate, w_up, w_down = weights
    live_rows, position, allowed = row_layout(lens_block, offs_block)
    cosine_tab, sine_tab = rope_tables(position)
    normed_one = low(row_vals * rms_scale(row_vals) * gain_one)
    query_raw = low_back(matmul_high(normed_one, w_query)).reshape(CAP, H, HD)
    key_raw = low_back(matmul_high(normed_one, w_key)).reshape(CAP, H, HD)
    value_bf = low(low_back(matmul_high(normed_one, w_value))).reshape(CAP, H, HD)
    query_rot = low(rotate(query_raw, cosine_tab, sine_tab))
    key_rot = low(rotate(key_raw, cosine_tab, sine_tab))
    raw_scores = 0.125 * jnp.einsum('qhd,khd->hqk', query_rot, key_rot, precision=lax.Precision.HIGHEST)
    scores = low_back(jnp.where(allowed[None], raw_scores, -1000000000.0))
    row_top = lax.optimization_barrier(jnp.max(scores, axis=2, keepdims=True))
    log_total = row_top + jnp.log(lax.optimization_barrier(jnp.sum(jnp.exp(scores - row_top), axis=2, keepdims=True)))
    attn_probs = jnp.exp(scores - log_total)
    mixed = jnp.einsum('hqk,khd->qhd', low(attn_probs), value_bf, precision=lax.Precision.HIGHEST)
    attended = low(low_back(mixed.reshape(CAP, H * HD)))
    resid = row_vals + live_rows * low_back(matmul_high(attended, w_out))
    normed_two = low(resid * rms_scale(resid) * gain_two)
    gate_pre = low_back(matmul_high(normed_two, w_gate))
    up_pre = low_back(matmul_high(normed_two, w_up))
    hidden = low(gate_pre * jax.nn.sigmoid(gate_pre) * up_pre)
    return resid + live_rows * low_back(matmul_high(hidden, w_down))

def forward(row_vals, weights, tile_len, tile_offset):
    blocks = (row_vals.reshape(N_DP, CAP, D), tile_len.reshape(N_DP, TILES_DEV), tile_offset.reshape(N_DP, TILES_DEV))
    result = lax.map(jax.checkpoint(partial(device_block, weights)), blocks)
    return result.reshape(TOKENS, D)

def reference(hidden_in, norm1_gain, w_query, w_key, w_value, w_out, norm2_gain, w_gate, w_up, w_down, tile_len, tile_offset, cotangent):
    weights = tuple((item.astype(jnp.float32) for item in (norm1_gain, w_query, w_key, w_value, w_out, norm2_gain, w_gate, w_up, w_down)))
    row_vals = hidden_in.astype(jnp.float32)
    result, pullback = jax.vjp(lambda rows_arg, weights_arg: forward(rows_arg, weights_arg, tile_len, tile_offset), row_vals, weights)
    row_grad, weight_grads = pullback(cotangent.astype(jnp.float32))
    return (result.astype(jnp.bfloat16), row_grad.astype(jnp.bfloat16), weight_grads[0], weight_grads[1], weight_grads[2], weight_grads[3], weight_grads[4], weight_grads[5], weight_grads[6], weight_grads[7], weight_grads[8])
```

```python
import functools
import math

import jax
import jax.numpy as jnp
from jax import lax
from jax.experimental import pallas as pl
from jax.experimental.pallas import tpu as pltpu
from jax.sharding import PartitionSpec as P

HD = 64
TILE = 128
BF = jnp.bfloat16
F32 = jnp.float32
CORE_PERM = [(0, 1), (1, 0), (2, 3), (3, 2)]
Y_PERM = [(0, 2), (2, 0), (1, 3), (3, 1)]
DIAG_PERM = [(0, 3), (3, 0), (1, 2), (2, 1)]
MIB = 1024 * 1024
T, C, Y, X, Z = range(5)


def dot(a, b):
    return lax.dot_general(a, b, (((1,), (0,)), ((), ())), preferred_element_type=F32)


def dot_rows(a, b):
    return lax.dot_general(a, b, (((0,), (0,)), ((), ())), preferred_element_type=F32)


def dot_t(a, b):
    return lax.dot_general(a, b, (((1,), (1,)), ((), ())), preferred_element_type=F32)


def core_go(a):
    return lax.ppermute(a, "tensor", CORE_PERM)


def y_go(a):
    return lax.ppermute(a, "tensor", Y_PERM)


def diag_go(a):
    return lax.ppermute(a, "tensor", DIAG_PERM)


def x_go(a):
    return lax.ppermute(a, "dp", [(i, i ^ 1) for i in range(lax.axis_size("dp"))])


def sds(shape, dtype=BF):
    return jax.ShapeDtypeStruct(shape, dtype)


def call(name, us, body, scal, grid, ins, outs, deps=(), scratch=(), aliases=None, limit=24, mark=False):
    n_in, n_dep, n_out = len(ins), len(deps), len(outs)
    if mark:
        outs = list(outs) + [(sds((8, 128), F32), (8, 128), fixed(0, 0))]

    def wrapped(s, *refs):
        if mark:
            refs[n_in + n_dep + n_out][...] = jnp.zeros((8, 128), F32)
            refs = refs[: n_in + n_dep + n_out] + refs[n_in + n_dep + n_out + 1 :]
        body(s, *refs[:n_in], *refs[n_in + n_dep :])

    spec = lambda block, index: pl.BlockSpec(memory_space=pl.ANY) if block is None else pl.BlockSpec(block, index)
    got = pl.pallas_call(
        wrapped,
        grid_spec=pltpu.PrefetchScalarGridSpec(
            num_scalar_prefetch=1,
            grid=grid,
            in_specs=[spec(b, i) for _, b, i in ins] + [pl.BlockSpec(memory_space=pl.ANY)] * n_dep,
            out_specs=[spec(b, i) for _, b, i in outs],
            scratch_shapes=list(scratch),
        ),
        out_shape=[o for o, _, _ in outs],
        input_output_aliases={k + 1: v for k, v in (aliases or {}).items()},
        compiler_params=pltpu.CompilerParams(vmem_limit_bytes=limit * MIB),
        cost_estimate=pl.CostEstimate(flops=int(us * 1.1e9), bytes_accessed=int(us * 3.6e6), transcendentals=0),
        name=name,
    )(scal, *[a for a, _, _ in ins], *deps)
    return got[0] if len(outs) == 1 else got


def fixed(*at):
    return lambda *_: at


def quarter_of(s, k):
    return 2 * lax.bitwise_xor(s[C], k % 2) + lax.bitwise_xor(s[Y], k // 2)


def swap_halves(v):
    width = v.shape[1]
    lane = lax.broadcasted_iota(jnp.int32, v.shape, 1) % HD
    return jnp.where(lane < HD // 2, pltpu.roll(v, width - HD // 2, 1), pltpu.roll(v, HD // 2, 1))


def widen(tab, width):
    return jnp.concatenate([tab] * (width // tab.shape[1]), axis=1)


def qkv_body(s, h0, h1, h2, h3, gain, wq, wk, wv, cos, sin, x_out, n_out, out):
    part = h0.shape[1]
    for k, h in enumerate((h0, h1, h2, h3)):
        at = pl.multiple_of(lax.bitwise_xor(s[T], k) * part, part)
        x_out[:, pl.ds(at, part)] = h[...]
    vals = x_out[...].astype(F32)
    inv = lax.rsqrt(jnp.mean(vals * vals, axis=1, keepdims=True) + 1e-05)
    n = (vals * inv * gain[...].astype(F32)).astype(BF)
    n_out[...] = n
    width = wq.shape[1]
    c, sn = widen(cos[...], 256), widen(sin[...], 256)
    for m, w in enumerate((wq, wk)):
        for at in range(0, width, 256):
            z = dot(n, w[:, at : at + 256])
            out[:, m * width + at : m * width + at + 256] = (z * c + swap_halves(z) * sn).astype(BF)
    for at in range(0, width, 256):
        out[:, 2 * width + at : 2 * width + at + 256] = dot(n, wv[:, at : at + 256]).astype(BF)


def qkv(scal, pieces, gain, wq, wk, wv, cos, sin, deps):
    slots, part = pieces[0].shape
    full, width = wq.shape
    blk = 256
    row = lambda i, s: (i, 0)
    return call(
        "qkv",
        14,
        qkv_body,
        scal,
        (slots // blk,),
        [(p, (blk, part), row) for p in pieces]
        + [(gain, (1, full), fixed(0, 0))]
        + [(w, (full, width), fixed(0, 0)) for w in (wq, wk, wv)]
        + [(cos, (blk, 128), row), (sin, (blk, 128), row)],
        [
            (sds((slots, full)), (blk, full), row),
            (sds((slots, full)), (blk, full), row),
            (sds((slots, 3 * width)), (blk, 3 * width), row),
        ],
        deps,
        limit=36,
    )


def mask_bias(seq_col, key_row, first, count):
    parts = []
    rows = seq_col[first : first + count, :]
    if first:
        parts.append(jnp.where(rows == key_row[:, :first], 0.0, -1e9))
    r = lax.broadcasted_iota(jnp.int32, (count, count), 0)
    c = lax.broadcasted_iota(jnp.int32, (count, count), 1)
    same = rows == key_row[:, first : first + count]
    parts.append(jnp.where((same & (c < r)) | (c == r), 0.0, -1e9))
    return parts[0] if len(parts) == 1 else jnp.concatenate(parts, axis=1)


def head_only(v, lane, h):
    return jnp.where(lane if h == 0 else jnp.logical_not(lane), v, jnp.zeros_like(v))


def attn_body(s, q_ref, k_ref, v_ref, seq_ref, key_ref, o_ref, lse_ref, *, blk):
    slots = q_ref.shape[0]
    lane = lax.broadcasted_iota(jnp.int32, (blk, 128), 1) < HD
    for i in range(slots // blk):
        first, n = i * blk, (i + 1) * blk
        bias = mask_bias(seq_ref, key_ref, first, blk)
        q2 = q_ref[first:n, :] * jnp.asarray(0.125, BF)
        k2 = k_ref[:n, :]
        v2 = v_ref[:n, :]
        outs, lses = [], []
        for h in range(2):
            sc = dot_t(head_only(q2, lane, h), k2) + bias
            top = jnp.max(sc, axis=1, keepdims=True)
            e = jnp.exp(sc - top)
            total = jnp.sum(e, axis=1, keepdims=True)
            outs.append(dot(e.astype(BF), v2) * (1.0 / total))
            lses.append(top + jnp.log(total))
        o_ref[first:n, :] = jnp.where(lane, outs[0], outs[1]).astype(BF)
        lse_ref[first:n, :] = jnp.where(lane, lses[0], lses[1])


def attention(scal, qkv_all, seq_col, key_row, deps):
    slots, width = qkv_all.shape
    width //= 3
    pairs = width // 128
    third = lambda m: lambda i, s: (0, m * pairs + i)
    return call(
        "attention",
        17,
        functools.partial(attn_body, blk=256),
        scal,
        (pairs,),
        [(qkv_all, (slots, 128), third(m)) for m in range(3)]
        + [(seq_col, (slots, 1), fixed(0, 0)), (key_row, (1, slots), fixed(0, 0))],
        [(sds((slots, width), d), (slots, 128), third(0)) for d in (BF, F32)],
        deps,
        limit=24,
    )


def attn_back_body(
    s, q_ref, k_ref, v_ref, o_ref, do_ref, lse_ref, seq_ref, key_ref, cos, sin, dq_ref, dk_ref, dv_ref, dk_acc, dv_acc, *, blk
):
    slots = q_ref.shape[0]
    lane = lax.broadcasted_iota(jnp.int32, (blk, 128), 1) < HD
    dk_acc[...] = jnp.zeros_like(dk_acc)
    dv_acc[...] = jnp.zeros_like(dv_acc)
    for i in range(slots // blk):
        first, n = i * blk, (i + 1) * blk
        bias = mask_bias(seq_ref, key_ref, first, blk)
        q2 = q_ref[first:n, :] * jnp.asarray(0.125, BF)
        do2 = do_ref[first:n, :]
        lse2 = lse_ref[first:n, :]
        prod = do2.astype(F32) * o_ref[first:n, :].astype(F32)
        k2 = k_ref[:n, :]
        v2 = v_ref[:n, :]
        dqs = []
        for h in range(2):
            qm = head_only(q2, lane, h)
            dom = head_only(do2, lane, h)
            delta = jnp.sum(head_only(prod, lane, h), axis=1, keepdims=True)
            p = jnp.exp(dot_t(qm, k2) + bias - lse2[:, h * HD : h * HD + 1])
            ds = (p * (dot_t(dom, v2) - delta)).astype(BF)
            dv_acc[:n, :] += dot_rows(p.astype(BF), dom)
            dk_acc[:n, :] += dot_rows(ds, qm)
            dqs.append(dot(ds, k2))
        dq = jnp.where(lane, dqs[0], dqs[1]) * 0.125
        dq_ref[first:n, :] = (dq * cos[first:n, :] - swap_halves(dq) * sin[first:n, :]).astype(BF)
    dk = dk_acc[...]
    dk_ref[...] = (dk * cos[...] - swap_halves(dk) * sin[...]).astype(BF)
    dv_ref[...] = dv_acc[...].astype(BF)


def attention_back(scal, half, qkv_all, o, do, lse, seq_col, key_row, cos, sin, deps):
    slots, width = o.shape
    pairs = width // 128
    count = pairs // 2
    third = lambda m: lambda i, s: (0, m * pairs + half * count + i)
    return call(
        "attention_back",
        13,
        functools.partial(attn_back_body, blk=256),
        scal,
        (count,),
        [(qkv_all, (slots, 128), third(m)) for m in range(3)]
        + [(a, (slots, 128), third(0)) for a in (o, do, lse)]
        + [(seq_col, (slots, 1), fixed(0, 0)), (key_row, (1, slots), fixed(0, 0))]
        + [(cos, (slots, 128), fixed(0, 0)), (sin, (slots, 128), fixed(0, 0))],
        [(sds((slots, width // 2)), (slots, 128), lambda i, s: (0, i))] * 3,
        deps,
        scratch=[pltpu.VMEM((slots, 128), F32)] * 2,
        limit=56,
    )


def tensor_body(s, *refs, n_pairs, op, mode):
    acc = None
    for p in range(n_pairs):
        term = op(refs[p][...], refs[n_pairs + p][...])
        acc = term if acc is None else acc + term
    rest = refs[2 * n_pairs :]
    if mode == "send":
        far, near = rest
        half = acc.shape[0] // 2
        low, high = acc[:half], acc[half:]
        far[...] = jnp.where(s[Y] == 0, high, low).astype(BF)
        near[...] = jnp.where(s[Y] == 0, low, high).astype(BF)
    else:
        got, out = rest
        out[...] = (acc + got[...].astype(F32)).astype(out.dtype)


def tensor_part(scal, mode, pairs, op, got, deps):
    slots = pairs[0][0].shape[0]
    quarter = slots // 4
    full = pairs[0][1].shape[1 if op is dot else 0]
    side = lambda at: lambda j, s: (j, at)
    tile = 512
    n_rows = 2 * quarter if mode == "send" else quarter
    row = {
        "send": lambda j, s: (1 - s[C], 0),
        "far": lambda j, s: (2 * s[C] + 1 - s[Y], 0),
        "near": lambda j, s: (2 * s[C] + s[Y], 0),
    }[mode]
    ins = [(a, (n_rows, a.shape[1]), row) for a, _, _ in pairs]
    for a, w, at in pairs:
        if op is dot:
            ins.append((w, (w.shape[0], tile), lambda j, s: (0, j)))
        else:
            ins.append((w, (tile, a.shape[1]), side(at)))
    col = lambda j, s: (0, j)
    if mode == "send":
        outs = [(sds((quarter, full)), (quarter, tile), col)] * 2
    else:
        ins.append((got, (quarter, tile), col))
        outs = [(sds((quarter, full), BF if mode == "far" else F32), (quarter, tile), col)]
    body = functools.partial(tensor_body, n_pairs=len(pairs), op=op, mode=mode)
    return call("tensor_" + mode, 5 if len(pairs) == 1 else 7, body, scal, (full // tile,), ins, outs, deps, limit=56)


def row_mean(v):
    return jnp.mean(v, axis=1, keepdims=True)


def own_quarter(g, s):
    return (quarter_of(s, 0), 0)


def back_of_norm(values, gain, upstream):
    inv = lax.rsqrt(row_mean(values * values) + 1e-05)
    gained = upstream * gain
    grad = jnp.sum(upstream * values * inv, axis=0, keepdims=True)
    return inv * gained - values * (inv * inv * inv) * row_mean(gained * values), grad


def joined(b0, from_x, from_y):
    return b0[...] + from_x[...].astype(F32) + from_y[...].astype(F32)


def norm2_back_body(s, b0, from_x, from_y, hres, live, gain, dm, da_out, back_out, grad_out):
    back, grad = back_of_norm(hres[...], gain[...].astype(F32), joined(b0, from_x, from_y))
    back_out[...] = back
    grad_out[...] = grad
    da_out[...] = (dm[...].astype(F32) + live[...] * back).astype(BF)


def norm2_back(scal, parts, hres, live, gain, dm, deps):
    rows, full = hres.shape
    whole = ((rows, full), fixed(0, 0))
    return call(
        "norm2_back", 7, norm2_back_body, scal, (1,),
        [(p, *whole) for p in parts]
        + [(hres, *whole), (live, (rows, 1), own_quarter), (gain, (1, full), fixed(0, 0)), (dm, *whole)],
        [(sds((rows, full)), *whole), (sds((rows, full), F32), *whole), (sds((1, full), F32), (1, full), fixed(0, 0))],
        deps,
    )


def feature_pieces(s, value, outs, hold):
    part = outs[0].shape[1]
    hold[...] = value.astype(BF)
    for k, out in enumerate(outs):
        out[...] = hold[:, pl.ds(pl.multiple_of(lax.bitwise_xor(s[T], k) * part, part), part)]


def norm1_back_body(s, near, back, x_own, gain, back_two, o0, o1, o2, o3, grad_out, hold):
    value, grad = back_of_norm(x_own[...].astype(F32), gain[...].astype(F32), near[...] + back[...].astype(F32))
    grad_out[...] = grad
    feature_pieces(s, value + back_two[...], (o0, o1, o2, o3), hold)


def norm1_back(scal, near, back, x_full, gain, back_two, deps):
    rows, full = near.shape
    whole = ((rows, full), fixed(0, 0))
    piece = (sds((rows, full // 4)), (rows, full // 4), fixed(0, 0))
    return call(
        "norm1_back", 6, norm1_back_body, scal, (1,),
        [(near, *whole), (back, *whole), (x_full, (rows, full), own_quarter), (gain, (1, full), fixed(0, 0)),
         (back_two, *whole)],
        [piece] * 4 + [(sds((1, full), F32), (1, full), fixed(0, 0))],
        deps,
        scratch=[pltpu.VMEM((rows, full), BF)],
        limit=56,
    )


def layer_body(s, b0, from_x, from_y, hres, live, o0, o1, o2, o3, hold):
    value = hres[...] + live[...] * joined(b0, from_x, from_y)
    feature_pieces(s, value, (o0, o1, o2, o3), hold)


def layer_rows(scal, parts, hres, live, deps):
    rows, full = hres.shape
    whole = ((rows, full), fixed(0, 0))
    piece = (sds((rows, full // 4)), (rows, full // 4), fixed(0, 0))
    return call(
        "layer_rows", 5, layer_body, scal, (1,),
        [(p, *whole) for p in parts]
        + [(hres, *whole), (live, (rows, 1), own_quarter)],
        [piece] * 4,
        deps,
        scratch=[pltpu.VMEM((rows, full), BF)],
    )


def place_body(s, *refs):
    out = refs[-1]
    rows = refs[0].shape[0]
    for k in range(4):
        at = pl.multiple_of(quarter_of(s, k) * rows, rows)
        value = refs[k][...]
        if len(refs) == 6:
            value = (value.astype(F32) + refs[4][pl.ds(at, rows), :].astype(F32)).astype(BF)
        out[pl.ds(at, rows), :] = value


def place_rows(scal, pieces, extra, deps):
    rows, cols = pieces[0].shape
    ins = [(p, (rows, cols), fixed(0, 0)) for p in pieces]
    if extra is not None:
        ins.append((extra, (4 * rows, cols), fixed(0, 0)))
    return call("place", 4, place_body, scal, (1,), ins, [(sds((4 * rows, cols)), (4 * rows, cols), fixed(0, 0))], deps)


def to_features(pieces):
    return [pieces[0], core_go(pieces[1]), y_go(pieces[2]), diag_go(pieces[3])]


def places():
    d, t = lax.axis_index("dp"), lax.axis_index("tensor")
    x, c, y = d % 2, t % 2, t // 2
    return x, c, y, {"tensor": t + 1 - 2 * c}, {"tensor": t + 2 - 4 * y}, {"dp": d + 1 - 2 * x}


def greet(*others):
    barrier = pltpu.get_barrier_semaphore()
    for other in others:
        pl.semaphore_signal(barrier, inc=1, device_id=other, device_id_type=pl.DeviceIdType.MESH)
    pl.semaphore_wait(barrier, len(others))


def remote(src, dst, send_sem, recv_sem, k, other):
    return pltpu.make_async_remote_copy(
        src_ref=src,
        dst_ref=dst,
        send_sem=send_sem.at[k],
        recv_sem=recv_sem.at[k],
        device_id=other,
        device_id_type=pl.DeviceIdType.MESH,
    )


def front_body(
    att, w_out, x_full, live, gain, dm0, dm0c, dmy, dmx, dmxc, wg, wu, wd,
    n2_out, hid_out, dga_out, dua_out, dm_out, down_out, hres_out,
    att_v, wo_v, xo_v, wg_v, wu_v, wd_v, n2_v, dm_v, snd, rcv, far_v, near_v, y_in, dyc, dxy, dxyc, hid_v, stage, sums,
    local, pieces_in, out_sem, whole_sem, sum_sem, send_sem, recv_sem,
):
    x, c, y, core, across_y, across_x = places()
    t = 2 * y + c
    rows, units, part = n2_v.shape[1], wg_v.shape[1], dmy.shape[1]

    def at(qc, qy):
        return pl.ds(pl.multiple_of((2 * qc + qy) * rows, rows), rows)

    def features(kc, ky):
        of = t + kc * (1 - 2 * c) + ky * (2 - 4 * y)
        return pl.ds(pl.multiple_of(of * part, part), part)

    dm_core = remote(dmy, dyc, send_sem, recv_sem, 3, core)
    dm_diag = remote(dmy, dxy, send_sem, recv_sem, 4, across_x)
    dm_on = remote(dxy, dxyc, send_sem, recv_sem, 5, core)
    half = pl.ds(pl.multiple_of(x * units, units), units)
    first = [
        pltpu.make_async_copy(att, att_v, local.at[0]),
        pltpu.make_async_copy(w_out, wo_v, local.at[1]),
        pltpu.make_async_copy(x_full.at[at(c, y), :], xo_v, local.at[2]),
    ]
    weights = [
        pltpu.make_async_copy(wg.at[:, half], wg_v, local.at[3]),
        pltpu.make_async_copy(wu.at[:, half], wu_v, local.at[4]),
        pltpu.make_async_copy(wd.at[half, :], wd_v, local.at[5]),
    ]
    for load in first:
        load.start()
    greet(core, across_y, across_x)
    dm_core.start()
    dm_diag.start()
    for load in weights:
        load.start()
    own_dm, pair_dm = [], []
    for r in range(8):
        ky, kx, kc = (r // 2) % 2, r // 4, r % 2
        from_rows = at(c + kc * (1 - 2 * c), y + ky * (1 - 2 * y))
        sources = ((dmx, 0, 0), (dmxc, 1, 0)) if kx else ((dm0, 0, 0), (dm0c, 1, 0), (dmy, 0, 1))
        for n, (source, fc, fy) in enumerate(sources):
            copy = pltpu.make_async_copy(
                source.at[from_rows, :], dm_v.at[r, :, features(fc, fy)], pieces_in.at[3 * r + n]
            )
            copy.start()
            (pair_dm if kx else own_dm).append(copy)

    for load in first:
        load.wait()

    def product(qc, qy, emit):
        left = att_v[at(qc, qy), :]
        for n in range(0, wo_v.shape[1], 256):
            emit(slice(n, n + 256), dot(left, wo_v[:, n : n + 256]))

    to_core = [remote(snd.at[k], rcv.at[k], send_sem, recv_sem, k, core) for k in range(2)]
    to_y = remote(far_v, y_in, send_sem, recv_sem, 2, across_y)
    for k, qy in enumerate((1 - y, y)):

        def put(cols, acc, k=k):
            snd[k, :, cols] = acc.astype(BF)

        product(1 - c, qy, put)
        to_core[k].start()
    to_core[0].wait_recv()

    def put_far(cols, acc):
        far_v[:, cols] = (acc + rcv[0, :, cols].astype(F32)).astype(BF)

    product(c, 1 - y, put_far)
    to_y.start()
    to_core[1].wait_recv()

    def put_near(cols, acc):
        near_v[:, cols] = acc + rcv[1, :, cols].astype(F32)

    product(c, y, put_near)
    for copy in own_dm:
        copy.wait()
    dm_core.wait_recv()
    for r in range(4):
        dm_v[r, :, features(1, 1)] = dyc[at(c + (r % 2) * (1 - 2 * c), y + (r // 2) * (1 - 2 * y)), :]

    to_y.wait_recv()
    hres = xo_v[...].astype(F32) + live[at(c, y), :] * (near_v[...] + y_in[...].astype(F32))
    hres_out[...] = hres
    n2_v[0] = (hres * lax.rsqrt(row_mean(hres * hres) + 1e-05) * gain[...].astype(F32)).astype(BF)

    def block_to(r_from, r_to, other):
        return remote(n2_v.at[r_from], n2_v.at[r_to], send_sem, recv_sem, 5 + r_to, other)

    n_y, n_x, n_c = block_to(0, 2, across_y), block_to(0, 4, across_x), block_to(0, 1, core)
    n_c.start()

    @pl.when(c == 0)
    def _():
        n_x.start()

    @pl.when(c == 1)
    def _():
        n_y.start()

    dm_diag.wait_recv()
    dm_on.start()
    for load in weights:
        load.wait()

    outs = (dga_out, dua_out)

    def order(i):
        inner = ((i + 2) // 4) % 2
        return i * (1 - inner) + inner * (2 + (2 * (1 - c) - i + 10) % 4)

    def store(i, k):
        place = pl.ds(pl.multiple_of(order(i) * rows, rows), rows)
        return pltpu.make_async_copy(stage.at[i % 2, k], outs[k].at[place, :], out_sem.at[i, k])

    def store_whole(i, source, out, k):
        place = pl.ds(pl.multiple_of(order(i) * rows, rows), rows)
        return pltpu.make_async_copy(source.at[order(i)], out.at[place, :], whole_sem.at[i, k])

    @pl.loop(0, 8)
    def _(i):
        r = order(i)

        @pl.when((i == 2) & (c == 0))
        def _():
            n_x.wait_send()
            n_y.start()
            n_x.wait_recv()
            block_to(4, 6, across_y).start()
            block_to(4, 5, core).start()

        @pl.when((i == 2) & (c == 1))
        def _():
            n_y.wait_send()
            n_x.start()
            n_y.wait_recv()
            block_to(2, 6, across_x).start()
            block_to(2, 3, core).start()

        @pl.when(i == 2)
        def _():
            for copy in pair_dm:
                copy.wait()
            dm_on.wait_recv()
            for b in range(4, 8):
                here = at(c + (b % 2) * (1 - 2 * c), y + ((b // 2) % 2) * (1 - 2 * y))
                dm_v[b, :, features(0, 1)] = dxy[here, :]
                dm_v[b, :, features(1, 1)] = dxyc[here, :]

        @pl.when((i == 4) & (c == 0))
        def _():
            n_y.wait_recv()
            block_to(2, 3, core).start()

        @pl.when((i == 4) & (c == 1))
        def _():
            n_x.wait_recv()
            block_to(4, 5, core).start()

        @pl.when((i == 1) | (i == 3) | (i == 5) | (i == 7))
        def _():
            block_to(0, r, core).wait_recv()

        @pl.when(i == 6)
        def _():
            block_to(2, 6, across_x).wait_recv()
            block_to(6, 7, core).start()

        store_whole(i, n2_v, n2_out, 0).start()
        store_whole(i, dm_v, dm_out, 1).start()

        @pl.when(i >= 2)
        def _():
            for k in range(2):
                store(i - 2, k).wait()

        for col in range(0, units, 256):
            cols = slice(col, col + 256)
            n = n2_v[r]
            ga = dot(n, wg_v[:, cols])
            ua = dot(n, wu_v[:, cols])
            dhid = dot_t(dm_v[r], wd_v[cols, :])
            sig = jax.nn.sigmoid(ga)
            silu = ga * sig
            hid_v[r, :, cols] = (silu * ua).astype(BF)
            stage[i % 2, 0, :, cols] = (dhid * ua * (sig * (1.0 + ga * (1.0 - sig)))).astype(BF)
            stage[i % 2, 1, :, cols] = (dhid * silu).astype(BF)
        for k in range(2):
            store(i, k).start()
        store_whole(i, hid_v, hid_out, 2).start()

    lines, width = sums.shape[1], sums.shape[3]

    def sum_store(u):
        here = pl.ds(pl.multiple_of(u * 256, 256), 256)
        return pltpu.make_async_copy(sums.at[u % 2], down_out.at[:, here, :], sum_sem.at[u])

    @pl.loop(0, units // 256)
    def _(u):
        @pl.when(u >= 2)
        def _():
            sum_store(u - 2).wait()

        turned = hid_v[:, :, pl.ds(pl.multiple_of(u * 256, 256), 256)].reshape(8 * rows, 256).T
        for n in range(0, lines * width, 256):
            value = dot(turned, dm_v[:, :, n : n + 256].reshape(8 * rows, 256)).astype(BF)
            piece = min(width, 256)
            for m in range(0, 256, piece):
                at_n = (n + m) % width
                sums[u % 2, (n + m) // width, :, at_n : at_n + piece] = value[:, m : m + piece]
        sum_store(u).start()

    for u in range(units // 256 - 2, units // 256):
        sum_store(u).wait()
    for i in (6, 7):
        for k in range(2):
            store(i, k).wait()

    @pl.loop(0, 8)
    def _(i):
        store_whole(i, n2_v, n2_out, 0).wait()
        store_whole(i, dm_v, dm_out, 1).wait()
        store_whole(i, hid_v, hid_out, 2).wait()

    @pl.when(c == 0)
    def _():
        n_y.wait_send()

    @pl.when(c == 1)
    def _():
        n_x.wait_send()

    for copy in (*to_core, to_y, dm_core, dm_diag, dm_on, n_c):
        copy.wait_send()
    for r_from, r_to in ((2, 3), (4, 5), (2, 6), (6, 7)):
        block_to(r_from, r_to, core).wait_send()


def front(att, w_out, x_full, live, gain, dm_pieces, wg, wu, wd, lines):
    slots, width = att.shape
    full = w_out.shape[1]
    rows, units, part = slots // 4, wg.shape[1] // 2, full // 4
    any_spec = pl.BlockSpec(memory_space=pl.ANY)
    vmem = pl.BlockSpec(memory_space=pltpu.VMEM)
    block = lambda *lead: pltpu.VMEM((*lead, rows, full), BF)
    piece = pltpu.VMEM((slots, part), BF)
    return pl.pallas_call(
        front_body,
        in_specs=[any_spec] * 3 + [vmem] * 2 + [any_spec] * 8,
        out_specs=[any_spec] * 6 + [vmem],
        out_shape=[sds((8 * rows, full))] + [sds((8 * rows, units))] * 3
        + [sds((8 * rows, full)), sds((lines, units, full // lines)), sds((rows, full), F32)],
        scratch_shapes=[
            pltpu.VMEM((slots, width), BF),
            pltpu.VMEM((width, full), BF),
            block(),
            pltpu.VMEM((full, units), BF),
            pltpu.VMEM((full, units), BF),
            pltpu.VMEM((units, full), BF),
            block(8),
            block(8),
            block(2),
            block(2),
            block(),
            pltpu.VMEM((rows, full), F32),
            block(),
            piece,
            piece,
            piece,
            pltpu.VMEM((8, rows, units), BF),
            pltpu.VMEM((2, 2, rows, units), BF),
            pltpu.VMEM((2, lines, 256, full // lines), BF),
            pltpu.SemaphoreType.DMA((6,)),
            pltpu.SemaphoreType.DMA((24,)),
            pltpu.SemaphoreType.DMA((8, 2)),
            pltpu.SemaphoreType.DMA((8, 3)),
            pltpu.SemaphoreType.DMA((units // 256,)),
            pltpu.SemaphoreType.DMA((13,)),
            pltpu.SemaphoreType.DMA((13,)),
        ],
        compiler_params=pltpu.CompilerParams(vmem_limit_bytes=62 * MIB, collective_id=2, has_side_effects=True),
        cost_estimate=pl.CostEstimate(flops=int(80 * 1.1e9), bytes_accessed=int(80 * 3.6e6), transcendentals=0),
        name="front",
    )(att, w_out, x_full, live, gain, *dm_pieces, wg, wu, wd)


def dn2_body(
    dga, dua, hid, wg, wu, wd, hres, dm, live, gain, da_out, back_out, grad_out, m_own, m_x, m_y,
    lefts, ws, wd_v, snd, rcv, kept, sb, via, via2, fx, fy, da_own, da_got, local, send_sem, recv_sem, credit,
):
    x, c, y, core, across_y, across_x = places()
    units, rows = wd_v.shape[0], snd.shape[1]
    half = pl.ds(pl.multiple_of(x * units, units), units)
    side = [slice(0, units), slice(units, 2 * units)]
    loads = [pltpu.make_async_copy(w.at[:, half], ws.at[:, side[p]], local.at[p]) for p, w in enumerate((wg, wu))]
    for kc in (1, 0):
        for p, left in enumerate((dga, dua)):
            loads.append(pltpu.make_async_copy(left.at[:, kc], lefts.at[kc, :, :, side[p]], local.at[2 + 2 * kc + p]))
    loads.append(pltpu.make_async_copy(hres, back_out, local.at[6]))
    loads.append(pltpu.make_async_copy(dm.at[pl.ds(0, rows), :], da_own, local.at[7]))
    loads.append(pltpu.make_async_copy(wd.at[half, :], wd_v, local.at[8]))
    hid_loads = [pltpu.make_async_copy(hid.at[:, kc], lefts.at[kc, :, :, side[0]], local.at[9 + kc]) for kc in range(2)]
    for load in loads:
        load.start()
    greet(core, across_y, across_x)
    for load in loads[:4]:
        load.wait()

    def tiles(kc, m, emit):
        for n in range(0, ws.shape[0], 256):
            emit(slice(n, n + 256), dot_t(lefts[kc, m], ws[n : n + 256, :]))

    def mlp_tiles(kc, m, emit):
        for n in range(0, wd_v.shape[1], 256):
            emit(slice(n, n + 256), dot(lefts[kc, m, :, :units], wd_v[:, n : n + 256]))

    def to_core(m, base):
        return remote(snd.at[m], rcv.at[m], send_sem, recv_sem, base + m, core)

    def send(m, make, base):
        def emit(cols, acc):
            snd[m, :, cols] = acc.astype(BF)

        make(1, m, emit)
        to_core(m, base).start()

    def keep(k, make, base):
        to_core(k, base).wait_recv()

        def emit(cols, acc):
            kept[k, :, cols] = acc + rcv[k, :, cols].astype(F32)

        make(0, k, emit)

    def diagonal_copy(dst, k, other):
        return remote(sb.at[0], dst, send_sem, recv_sem, k, other)

    def send_diagonal(dst, k):
        sb[0] = kept[3].astype(BF)

        @pl.when(c == 0)
        def _():
            diagonal_copy(dst, k, across_x).start()

        @pl.when(c == 1)
        def _():
            diagonal_copy(dst, k, across_y).start()

    @pl.loop(0, 4)
    def _(m):
        send(3 - m, tiles, 0)

    for load in loads[4:]:
        load.wait()
    go_x = remote(sb.at[1], fx, send_sem, recv_sem, 5, across_x)
    go_y = remote(sb.at[2], fy, send_sem, recv_sem, 6, across_y)

    @pl.loop(0, 4)
    def _(i):
        keep(3 - i, tiles, 0)

        @pl.when(i == 0)
        def _():
            send_diagonal(via, 4)

        @pl.when((i == 1) & (c == 0))
        def _():
            sb[1] = kept[2].astype(BF)
            go_x.start()

        @pl.when((i == 2) & (c == 1))
        def _():
            sb[2] = kept[1].astype(BF)
            go_y.start()

    pl.semaphore_signal(credit, inc=1, device_id=core, device_id_type=pl.DeviceIdType.MESH)
    for load in hid_loads:
        load.start()
    cf = c.astype(F32)
    diagonal_copy(via, 4, across_x).wait_recv()

    @pl.when(c == 1)
    def _():
        sb[1] = (kept[2] + via[...].astype(F32)).astype(BF)
        go_x.start()

    @pl.when(c == 0)
    def _():
        sb[2] = (kept[1] + via[...].astype(F32)).astype(BF)
        go_y.start()

    @pl.loop(0, 4)
    def _(m):
        to_core(m, 0).wait_send()

    pl.semaphore_wait(credit, 1)
    for load in hid_loads:
        load.wait()

    @pl.loop(0, 4)
    def _(m):
        send(3 - m, mlp_tiles, 10)

    go_x.wait_recv()
    go_y.wait_recv()
    dn2 = kept[0] + fx[...].astype(F32) + fy[...].astype(F32)
    back, grad = back_of_norm(back_out[...], gain[...].astype(F32), dn2)
    back_out[...] = back
    grad_out[...] = grad

    def at(qc, qy):
        return pl.ds(pl.multiple_of((2 * qc + qy) * rows, rows), rows)

    da_own[...] = (da_own[...].astype(F32) + live[at(c, y), :] * back).astype(BF)
    to_y = remote(da_own, da_got.at[1], send_sem, recv_sem, 8, across_y)
    to_c = remote(da_own, da_got.at[0], send_sem, recv_sem, 7, core)
    on = remote(da_got.at[1], da_got.at[2], send_sem, recv_sem, 9, core)
    to_y.start()
    to_c.start()
    da_out[at(c, y), :] = da_own[...]

    diagonal_copy(via, 4, across_x).wait_send()

    @pl.loop(0, 4)
    def _(i):
        keep(3 - i, mlp_tiles, 10)

        @pl.when(i == 0)
        def _():
            send_diagonal(via2, 14)

    for copy in (go_x, go_y):
        copy.wait_send()
    diagonal_copy(via2, 14, across_x).wait_recv()
    sb[1] = (kept[2] + cf * via2[...].astype(F32)).astype(BF)
    sb[2] = (kept[1] + (1.0 - cf) * via2[...].astype(F32)).astype(BF)
    stores = [
        pltpu.make_async_copy(source, out, local.at[11 + k])
        for k, (source, out) in enumerate(((kept.at[0], m_own), (sb.at[1], m_x), (sb.at[2], m_y)))
    ]
    for store in stores:
        store.start()
    to_c.wait_recv()
    da_out[at(1 - c, y), :] = da_got[0]
    to_y.wait_recv()
    on.start()
    da_out[at(c, 1 - y), :] = da_got[1]
    on.wait_recv()
    da_out[at(1 - c, 1 - y), :] = da_got[2]
    for store in stores:
        store.wait()

    @pl.loop(0, 4)
    def _(m):
        to_core(m, 10).wait_send()

    diagonal_copy(via2, 14, across_x).wait_send()
    for copy in (to_y, to_c, on):
        copy.wait_send()


def dn2_sum(dga, dua, hid, wg, wu, wd, hres, dm, live, gain, deps):
    tokens, units = dga.shape
    full = wg.shape[0]
    rows = tokens // 8
    slots = 4 * rows
    n_dep = len(deps)
    any_spec = pl.BlockSpec(memory_space=pl.ANY)
    vmem = pl.BlockSpec(memory_space=pltpu.VMEM)

    def body(*refs):
        dn2_body(*refs[:10], *refs[10 + n_dep :])

    block = lambda *lead: pltpu.VMEM((*lead, rows, full), BF)
    lefts = [v.reshape(4, 2, rows, units) for v in (dga, dua, hid)]
    return pl.pallas_call(
        body,
        in_specs=[any_spec] * 8 + [vmem] * 2 + [any_spec] * n_dep,
        out_specs=[vmem] * 3 + [any_spec] * 3,
        out_shape=[sds((slots, full)), sds((rows, full), F32), sds((1, full), F32), sds((rows, full), F32)]
        + [sds((rows, full))] * 2,
        scratch_shapes=[
            pltpu.VMEM((2, 4, rows, 2 * units), BF),
            pltpu.VMEM((full, 2 * units), BF),
            pltpu.VMEM((units, full), BF),
            block(4),
            block(4),
            pltpu.VMEM((4, rows, full), F32),
            block(3),
            block(),
            block(),
            block(),
            block(),
            block(),
            block(3),
            pltpu.SemaphoreType.DMA((14,)),
            pltpu.SemaphoreType.DMA((15,)),
            pltpu.SemaphoreType.DMA((15,)),
            pltpu.SemaphoreType.REGULAR,
        ],
        compiler_params=pltpu.CompilerParams(vmem_limit_bytes=62 * MIB, collective_id=1, has_side_effects=True),
        cost_estimate=pl.CostEstimate(flops=int(95 * 1.1e9), bytes_accessed=int(95 * 3.6e6), transcendentals=0),
        name="dn2_sum",
    )(*lefts, wg, wu, wd, hres, dm, live, gain, *deps)


def grad_body(s, a, b, *refs):
    out = refs[-1]
    a_t = a[...].T
    for col in range(0, b.shape[1], 256):
        out[0, :, col : col + 256] = dot(a_t, b[:, col : col + 256]).astype(BF)


def grad_by_rows(scal, a, b, lines, slot, slots, into, deps):
    tokens, m = a.shape
    n = b.shape[1]
    tile = min(256, m // lines)
    per = m // lines // tile
    ins = [(a, (tokens, tile), lambda j, s: (0, j)), (b, b.shape, fixed(0, 0))]
    if into is not None:
        ins.append((into, None, None))
    out = (sds((lines, m // lines, slots * n)), (1, tile, n), lambda j, s: (j // per, j % per, slot))
    aliases = None if into is None else {2: 0}
    return call("grad", 14, grad_body, scal, (m // tile,), ins, [out], deps, aliases=aliases, limit=56)


def line_sum(parts):
    n_dp = lax.axis_size("dp")
    groups = [[2 * z + x for z in range(n_dp // 2)] for x in range(2)]
    return lax.psum_scatter(parts, "dp", scatter_dimension=0, axis_index_groups=groups, tiled=False)


def pair_grad_body(s, a, *refs, n_b, keep):
    a_t = a[...].T
    out = refs[-1]
    width = refs[0].shape[1]
    for k in range(n_b):
        for col in range(0, width, 256):
            value = dot(a_t, refs[k][:, col : col + 256])
            at = k * width + col
            if keep:
                value = value + refs[n_b][0, :, at : at + 256].astype(F32)
            out[0, :, at : at + 256] = value.astype(BF)
    if n_b * width < out.shape[2]:
        out[0, :, n_b * width :] = refs[n_b + 1][0]


def pair_grad(scal, a, bs, lines, got, deps, extra=None):
    rows = a.shape[1] // (2 * lines)
    keep = got is not None
    member = (lambda s: s[X]) if keep else (lambda s: 1 - s[X])
    ins = [(a, (a.shape[0], rows), lambda j, s: (0, 2 * j + member(s)))]
    ins += [(b, b.shape, fixed(0, 0)) for b in bs]
    shard = lambda j, s: (j, 0, 0)
    total = bs[0].shape[1] * len(bs)
    for more in (got, extra):
        if more is not None:
            ins.append((more, (1, rows, more.shape[2]), shard))
    if extra is not None:
        total += extra.shape[2]
    outs = [(sds((lines, rows, total)), (1, rows, total), shard)]
    body = functools.partial(pair_grad_body, n_b=len(bs), keep=keep)
    name = "pair_grad_keep" if keep else "pair_grad_send"
    return call(name, 4 + total // 512, body, scal, (lines,), ins, outs, deps, limit=56)


def flip_body(s, total, out):
    out[...] = total[...].astype(F32).T


def flip(scal, total, first, width, deps):
    rows = total.shape[0]
    part = math.gcd(first, width)
    at = first // part
    return call(
        "flip", 3, flip_body, scal, (width // part,), [(total, (rows, part), lambda g, s: (0, at + g))],
        [(sds((width, rows), F32), (part, rows), lambda g, s: (g, 0))], deps,
    )


def halves_body(s, first, last, *outs):
    part = outs[0].shape[1] // 2
    for k, out in enumerate(outs):
        cols = slice(k * part, (k + 1) * part)
        out[:, :part] = first[:, cols].astype(F32)
        out[:, part:] = last[:, cols].astype(F32)


def head_halves(scal, first, last, part, deps):
    rows = first.shape[0]
    out = (sds((rows, 2 * part), F32), (rows, 2 * part), fixed(0, 0))
    return call(
        "head_halves", 3, halves_body, scal, (1,), [(v, v.shape, fixed(0, 0)) for v in (first, last)], [out] * 3, deps
    )


def pick(s, value, axis, other):
    half = value.shape[axis] // 2
    low, high = (value[:half], value[half:]) if axis == 0 else (value[:, :half], value[:, half:])
    return jnp.where(s[X] == (1 if other else 0), low, high)


def pair_send_body(s, total, out, *, axis):
    out[...] = pick(s, total[...], axis, True)


def pair_send(scal, total, axis, deps):
    shape = tuple(n // 2 if k == axis else n for k, n in enumerate(total.shape))
    body = functools.partial(pair_send_body, axis=axis)
    return call("pair_send", 3, body, scal, (1,), [(total, total.shape, fixed(0, 0))], [(sds(shape), shape, fixed(0, 0))], deps)


def hold_body(s, value, out):
    out[...] = value[...]


def hold(scal, value, deps):
    whole = (value.shape, fixed(0, 0))
    return call("hold", 2, hold_body, scal, (1,), [(value, *whole)], [(sds(value.shape), *whole)], deps)


def pair_join_body(s, total, got, *outs, axis):
    mine = pl.program_id(0) == s[X]
    width = got.shape[1] // len(outs)
    own = pick(s, total[...], axis, False)
    for k, out in enumerate(outs):
        cols = slice(k * width, (k + 1) * width)
        out[...] = jnp.where(mine, own[:, cols], got[:, cols]).astype(F32)


def pair_join(scal, total, got, axis, n_out, deps):
    rows, cols = got.shape
    cols //= n_out
    shape = (rows, 2 * cols) if axis == 0 else (2 * rows, cols)
    place = (lambda g, s: (0, g)) if axis == 0 else (lambda g, s: (g, 0))
    body = functools.partial(pair_join_body, axis=axis)
    return call(
        "pair_join", 4, body, scal, (2,),
        [(total, total.shape, fixed(0, 0)), (got, got.shape, fixed(0, 0))],
        [(sds(shape, F32), (rows, cols), place)] * n_out,
        deps,
    )


def gains_body(one, two, out, have, got, send_sem, recv_sem, *, lines):
    x, c, y, core, across_y, across_x = places()
    z = lax.axis_index("dp") // 2
    along = [{"dp": 2 * ((z + s) % lines) + x} for s in range(1, lines)]
    greet(core, across_y, across_x, *along)
    have[0, 0:1, :] = one[...]
    have[0, 1:2, :] = two[...]
    copies = []
    for k, other in enumerate((core, across_y, across_x)):
        copy = remote(have.at[k], got.at[k], send_sem, recv_sem, k, other)
        copy.start()
        copy.wait_recv()
        have[k + 1] = have[k] + got[k]
        copies.append(copy)
    last = [remote(have.at[3], got.at[3 + s], send_sem, recv_sem, 3 + s, other) for s, other in enumerate(along)]
    for copy in last:
        copy.start()
    total = have[3]
    for s, copy in enumerate(last):
        copy.wait_recv()
        total = total + got[3 + s]
    out[...] = total
    for copy in copies + last:
        copy.wait_send()


def gains_sum(one, two, lines, deps):
    full = one.shape[1]
    vmem = pl.BlockSpec(memory_space=pltpu.VMEM)
    n = 2 + lines

    def body(one, two, *refs):
        gains_body(one, two, *refs[len(deps) :], lines=lines)

    return pl.pallas_call(
        body,
        in_specs=[vmem] * 2 + [pl.BlockSpec(memory_space=pl.ANY)] * len(deps),
        out_specs=vmem,
        out_shape=sds((2, full), F32),
        scratch_shapes=[
            pltpu.VMEM((4, 2, full), F32),
            pltpu.VMEM((n, 2, full), F32),
            pltpu.SemaphoreType.DMA((n,)),
            pltpu.SemaphoreType.DMA((n,)),
        ],
        compiler_params=pltpu.CompilerParams(vmem_limit_bytes=24 * MIB, collective_id=3, has_side_effects=True),
        cost_estimate=pl.CostEstimate(flops=int(12 * 1.1e9), bytes_accessed=int(12 * 3.6e6), transcendentals=0),
        name="gains",
    )(one, two, *deps)


def layout(tile_len, tile_offset):
    tiles = tile_len.shape[0]
    within = jnp.arange(TILE, dtype=jnp.int32)[None, :]
    live = within < tile_len[:, None]
    position = (tile_offset[:, None] * TILE + within).astype(F32)
    seq = jnp.cumsum((tile_offset == 0).astype(jnp.int32))
    seq = jnp.broadcast_to(seq[:, None], (tiles, TILE))
    key = jnp.where(live, seq, -1)
    slots = tiles * TILE
    return live.astype(F32).reshape(slots, 1), position.reshape(slots), seq.reshape(slots, 1), key.reshape(1, slots)


def rope_tables(position):
    frequency = jnp.power(130000.0, -2.0 * jnp.arange(HD // 2, dtype=F32) / HD)
    angles = position[:, None] * frequency[None, :]
    c, s = jnp.cos(angles), jnp.sin(angles)
    return jnp.concatenate([c, c, c, c], axis=1), jnp.concatenate([-s, s, -s, s], axis=1)


def gather_tensor(own):
    far = y_go(own)
    return [own, core_go(own), far, core_go(far)]


def shards(
    hidden_in,
    norm1_gain,
    w_query,
    w_key,
    w_value,
    w_out,
    norm2_gain,
    w_gate,
    w_up,
    w_down,
    tile_len,
    tile_offset,
    cotangent,
):
    n_dp = lax.axis_size("dp")
    lines = n_dp // 2
    d, t = lax.axis_index("dp").astype(jnp.int32), lax.axis_index("tensor").astype(jnp.int32)
    zz, xx = d // 2, d % 2
    yy, cc = t // 2, t % 2
    scal = jnp.stack([t, cc, yy, xx, zz])
    full = w_query.shape[0]
    rows_dp = full // n_dp
    gain_one, gain_two = norm1_gain[None, :], norm2_gain[None, :]
    live, position, seq_col, key_row = layout(tile_len, tile_offset)
    cos, sin = rope_tables(position)

    pieces = gather_tensor(hidden_in)
    dm_own = (cotangent.astype(F32) * live).astype(BF)
    dm_x = x_go(dm_own)
    dm_pieces = [dm_own, core_go(dm_own), y_go(dm_own), dm_x, core_go(dm_x)]

    x_full, n1, qkv_all = qkv(scal, pieces, gain_one, w_query, w_key, w_value, cos, sin, ())
    attended, lse = attention(scal, qkv_all, seq_col, key_row, ())
    n2, hid, dga, dua, dm, down_parts, hres = front(
        attended, w_out, x_full, live, gain_two, dm_pieces, w_gate, w_up, w_down, lines
    )

    narrow = rows_dp % 128 == 0
    down_sum = line_sum(down_parts)
    gate_up = grad_by_rows(scal, n2, dga, lines, 0, 2, None, ())
    gate_up = grad_by_rows(scal, n2, dua, lines, 1, 2, gate_up, ())
    ups_sum = line_sum(gate_up)
    da, back_two, grad_two, m_own, m_x, m_y = dn2_sum(
        dga, dua, hid, w_gate, w_up, w_down, hres, dm, live, gain_two, (gate_up,)
    )
    dob = dob_rows(scal, da, w_out, ())
    back_args = (qkv_all, attended, dob, lse, seq_col, key_row, cos, sin)
    if narrow:
        out_sent = pair_grad(scal, da, [attended], lines, None, (dob,))
        out_got = x_go(out_sent)
        back_a = attention_back(scal, 0, *back_args, (out_sent,))
        sent_a = pair_grad(scal, n1, back_a, lines, None, ())
        got_a = x_go(sent_a)
        m_x = hold(scal, m_x, (sent_a,))
        back_b = attention_back(scal, 1, *back_args, (m_x,))
        sent_b = pair_grad(scal, n1, back_b, lines, None, ())
        got_b = x_go(sent_b)
        out_parts = pair_grad(scal, da, [attended], lines, out_got, (sent_b,))
        last = out_parts
    else:
        back_a = attention_back(scal, 0, *back_args, ())
        back_b = attention_back(scal, 1, *back_args, ())
        last = back_b[0]
    if narrow:
        first_parts = pair_grad(scal, n1, back_a, lines, got_a, (last,), out_parts)
        last = first_parts
    layer_parts = layer_rows(scal, (m_own, x_go(m_x), y_go(m_y)), hres, live, (last,))
    layer_pieces = to_features(layer_parts)
    last = layer_parts[0]
    dn1_pairs = [(v, w, k) for k, back in enumerate((back_a, back_b)) for v, w in zip(back, (w_query, w_key, w_value))]
    send_far, send_near = tensor_part(scal, "send", dn1_pairs, dot_t, None, (last,))
    far = tensor_part(scal, "far", dn1_pairs, dot_t, core_go(send_far), ())
    down_send = pair_send(scal, down_sum, 1, (far,))
    ups_send = pair_send(scal, ups_sum, 0, (down_send,))
    layer_out = place_rows(scal, layer_pieces, None, (ups_send,))
    near = tensor_part(scal, "near", dn1_pairs, dot_t, core_go(send_near), (layer_out,))
    last = near
    if narrow:
        last_parts = pair_grad(scal, n1, back_b, lines, got_b, (near,))
        last = last_parts
    else:
        *first, out_parts = wide_pair_grads(xx, [(n1, v) for v in back_a] + [(da, attended)], lines)
        first_parts = jnp.concatenate(first + [out_parts], axis=2)
        last_parts = jnp.concatenate(wide_pair_grads(xx, [(n1, v) for v in back_b], lines), axis=2)
    first_sum, last_sum = line_sum(first_parts), line_sum(last_parts)
    *in_parts, grad_one = norm1_back(scal, near, y_go(far), x_full, gain_one, back_two, (last,))
    in_pieces = to_features(in_parts)
    all_gains = gains_sum(grad_one, grad_two, lines, ())
    gate_grad, up_grad = pair_join(scal, ups_sum, x_go(ups_send), 0, 2, (all_gains,))
    down_grad = pair_join(scal, down_sum, x_go(down_send), 1, 1, (gate_grad,))
    gains = lax.dynamic_slice_in_dim(all_gains, d * rows_dp, rows_dp, 1)
    part = back_a[0].shape[1]
    out_grad = flip(scal, first_sum, 3 * part, 2 * part, (down_grad,))
    input_grad = place_rows(scal, in_pieces, cotangent, (out_grad,))
    query_grad, key_grad, value_grad = head_halves(scal, first_sum, last_sum, part, (input_grad,))
    return (
        layer_out,
        input_grad,
        gains[0],
        query_grad,
        key_grad,
        value_grad,
        out_grad,
        gains[1],
        gate_grad,
        up_grad,
        down_grad,
    )


def dob_body(s, da, w, out):
    out[...] = dot_t(da[...], w[...]).astype(BF)


def dob_rows(scal, da, w_out, deps):
    slots, full = da.shape
    width = w_out.shape[0]
    blk = 512
    return call(
        "dob", 6, dob_body, scal, (slots // blk,),
        [(da, (blk, full), lambda i, s: (i, 0)), (w_out, (width, full), fixed(0, 0))],
        [(sds((slots, width)), (blk, width), lambda i, s: (i, 0))],
        deps,
    )


def wide_pair_grads(xx, pairs, lines):
    sums = []
    for a, b in pairs:
        parts = dot_rows(a, b).astype(BF)
        parts = parts.reshape(lines, 2, parts.shape[0] // (2 * lines), parts.shape[1])
        got = x_go(lax.dynamic_index_in_dim(parts, 1 - xx, 1, keepdims=False))
        keep = lax.dynamic_index_in_dim(parts, xx, 1, keepdims=False)
        sums.append((keep.astype(F32) + got.astype(F32)).astype(BF))
    return sums


def solution(mesh):
    in_specs = (
        P("dp", "tensor"),
        P(),
        P(None, "tensor"),
        P(None, "tensor"),
        P(None, "tensor"),
        P("tensor", None),
        P(),
        P(None, "tensor"),
        P(None, "tensor"),
        P("tensor", None),
        P("dp"),
        P("dp"),
        P("dp", "tensor"),
    )
    out_specs = (
        P("dp", "tensor"),
        P("dp", "tensor"),
        P("dp"),
        P("dp", "tensor"),
        P("dp", "tensor"),
        P("dp", "tensor"),
        P("tensor", "dp"),
        P("dp"),
        P("dp", "tensor"),
        P("dp", "tensor"),
        P("tensor", "dp"),
    )
    return jax.shard_map(shards, mesh=mesh, in_specs=in_specs, out_specs=out_specs, check_vma=False)
```

```python
import functools
import math

import jax
import jax.numpy as jnp
from jax import lax
from jax.experimental import pallas as pl
from jax.experimental.pallas import tpu as pltpu
from jax.sharding import PartitionSpec as P

HD = 64
TILE = 128
BF = jnp.bfloat16
F32 = jnp.float32
CORE_PERM = [(0, 1), (1, 0), (2, 3), (3, 2)]
Y_PERM = [(0, 2), (2, 0), (1, 3), (3, 1)]
DIAG_PERM = [(0, 3), (3, 0), (1, 2), (2, 1)]
MIB = 1024 * 1024
T, C, Y, X, Z = range(5)


def dot(a, b):
    return lax.dot_general(a, b, (((1,), (0,)), ((), ())), preferred_element_type=F32)


def dot_rows(a, b):
    return lax.dot_general(a, b, (((0,), (0,)), ((), ())), preferred_element_type=F32)


def dot_t(a, b):
    return lax.dot_general(a, b, (((1,), (1,)), ((), ())), preferred_element_type=F32)


def core_go(a):
    return lax.ppermute(a, "tensor", CORE_PERM)


def y_go(a):
    return lax.ppermute(a, "tensor", Y_PERM)


def diag_go(a):
    return lax.ppermute(a, "tensor", DIAG_PERM)


def x_go(a):
    return lax.ppermute(a, "dp", [(i, i ^ 1) for i in range(lax.axis_size("dp"))])


def sds(shape, dtype=BF):
    return jax.ShapeDtypeStruct(shape, dtype)


def call(name, us, body, scal, grid, ins, outs, deps=(), scratch=(), aliases=None, limit=24, mark=False):
    n_in, n_dep, n_out = len(ins), len(deps), len(outs)
    if mark:
        outs = list(outs) + [(sds((8, 128), F32), (8, 128), fixed(0, 0))]

    def wrapped(s, *refs):
        if mark:
            refs[n_in + n_dep + n_out][...] = jnp.zeros((8, 128), F32)
            refs = refs[: n_in + n_dep + n_out] + refs[n_in + n_dep + n_out + 1 :]
        body(s, *refs[:n_in], *refs[n_in + n_dep :])

    spec = lambda block, index: pl.BlockSpec(memory_space=pl.ANY) if block is None else pl.BlockSpec(block, index)
    got = pl.pallas_call(
        wrapped,
        grid_spec=pltpu.PrefetchScalarGridSpec(
            num_scalar_prefetch=1,
            grid=grid,
            in_specs=[spec(b, i) for _, b, i in ins] + [pl.BlockSpec(memory_space=pl.ANY)] * n_dep,
            out_specs=[spec(b, i) for _, b, i in outs],
            scratch_shapes=list(scratch),
        ),
        out_shape=[o for o, _, _ in outs],
        input_output_aliases={k + 1: v for k, v in (aliases or {}).items()},
        compiler_params=pltpu.CompilerParams(vmem_limit_bytes=limit * MIB),
        cost_estimate=pl.CostEstimate(flops=int(us * 1.1e9), bytes_accessed=int(us * 3.6e6), transcendentals=0),
        name=name,
    )(scal, *[a for a, _, _ in ins], *deps)
    return got[0] if len(outs) == 1 else got


def fixed(*at):
    return lambda *_: at


def quarter_of(s, k):
    return 2 * lax.bitwise_xor(s[C], k % 2) + lax.bitwise_xor(s[Y], k // 2)


def swap_halves(v):
    width = v.shape[1]
    lane = lax.broadcasted_iota(jnp.int32, v.shape, 1) % HD
    return jnp.where(lane < HD // 2, pltpu.roll(v, width - HD // 2, 1), pltpu.roll(v, HD // 2, 1))


def widen(tab, width):
    return jnp.concatenate([tab] * (width // tab.shape[1]), axis=1)


def qkv_body(s, h0, h1, h2, h3, gain, wq, wk, wv, cos, sin, x_out, n_out, out):
    part = h0.shape[1]
    for k, h in enumerate((h0, h1, h2, h3)):
        at = pl.multiple_of(lax.bitwise_xor(s[T], k) * part, part)
        x_out[:, pl.ds(at, part)] = h[...]
    vals = x_out[...].astype(F32)
    inv = lax.rsqrt(jnp.mean(vals * vals, axis=1, keepdims=True) + 1e-05)
    n = (vals * inv * gain[...].astype(F32)).astype(BF)
    n_out[...] = n
    width = wq.shape[1]
    c, sn = widen(cos[...], 256), widen(sin[...], 256)
    for m, w in enumerate((wq, wk)):
        for at in range(0, width, 256):
            z = dot(n, w[:, at : at + 256])
            out[:, m * width + at : m * width + at + 256] = (z * c + swap_halves(z) * sn).astype(BF)
    for at in range(0, width, 256):
        out[:, 2 * width + at : 2 * width + at + 256] = dot(n, wv[:, at : at + 256]).astype(BF)


def qkv(scal, pieces, gain, wq, wk, wv, cos, sin, deps):
    slots, part = pieces[0].shape
    full, width = wq.shape
    blk = 256
    row = lambda i, s: (i, 0)
    return call(
        "qkv",
        14,
        qkv_body,
        scal,
        (slots // blk,),
        [(p, (blk, part), row) for p in pieces]
        + [(gain, (1, full), fixed(0, 0))]
        + [(w, (full, width), fixed(0, 0)) for w in (wq, wk, wv)]
        + [(cos, (blk, 128), row), (sin, (blk, 128), row)],
        [
            (sds((slots, full)), (blk, full), row),
            (sds((slots, full)), (blk, full), row),
            (sds((slots, 3 * width)), (blk, 3 * width), row),
        ],
        deps,
        limit=36,
    )


def mask_bias(seq_col, key_row, first, count):
    parts = []
    rows = seq_col[first : first + count, :]
    if first:
        parts.append(jnp.where(rows == key_row[:, :first], 0.0, -1e9))
    r = lax.broadcasted_iota(jnp.int32, (count, count), 0)
    c = lax.broadcasted_iota(jnp.int32, (count, count), 1)
    same = rows == key_row[:, first : first + count]
    parts.append(jnp.where((same & (c < r)) | (c == r), 0.0, -1e9))
    return parts[0] if len(parts) == 1 else jnp.concatenate(parts, axis=1)


def head_only(v, lane, h):
    return jnp.where(lane if h == 0 else jnp.logical_not(lane), v, jnp.zeros_like(v))


def attn_body(s, q_ref, k_ref, v_ref, seq_ref, key_ref, o_ref, lse_ref, mask, *, blk):
    slots = q_ref.shape[0]

    @pl.when(pl.program_id(0) == 0)
    def _():
        for first in range(0, slots, blk):
            mask[first : first + blk, : first + blk] = mask_bias(seq_ref, key_ref, first, blk)

    lane = lax.broadcasted_iota(jnp.int32, (blk, 128), 1) < HD
    for i in range(slots // blk):
        first, n = i * blk, (i + 1) * blk
        bias = mask[first:n, :n]
        q2 = q_ref[first:n, :] * jnp.asarray(0.125, BF)
        k2 = k_ref[:n, :]
        v2 = v_ref[:n, :]
        outs, lses = [], []
        for h in range(2):
            sc = dot_t(head_only(q2, lane, h), k2) + bias
            top = jnp.max(sc, axis=1, keepdims=True)
            e = jnp.exp(sc - top)
            total = jnp.sum(e, axis=1, keepdims=True)
            outs.append(dot(e.astype(BF), v2) * (1.0 / total))
            lses.append(top + jnp.log(total))
        o_ref[first:n, :] = jnp.where(lane, outs[0], outs[1]).astype(BF)
        lse_ref[first:n, :] = jnp.where(lane, lses[0], lses[1])


def attention(scal, qkv_all, seq_col, key_row, deps):
    slots, width = qkv_all.shape
    width //= 3
    pairs = width // 128
    third = lambda m: lambda i, s: (0, m * pairs + i)
    return call(
        "attention",
        17,
        functools.partial(attn_body, blk=256),
        scal,
        (pairs,),
        [(qkv_all, (slots, 128), third(m)) for m in range(3)]
        + [(seq_col, (slots, 1), fixed(0, 0)), (key_row, (1, slots), fixed(0, 0))],
        [(sds((slots, width), d), (slots, 128), third(0)) for d in (BF, F32)],
        deps,
        scratch=[pltpu.VMEM((slots, slots), F32)],
        limit=24,
    )


def attn_back_body(
    s, q_ref, k_ref, v_ref, o_ref, do_ref, lse_ref, seq_ref, key_ref, cos, sin, dq_ref, dk_ref, dv_ref, dk_acc, dv_acc, *, blk
):
    slots = q_ref.shape[0]
    lane = lax.broadcasted_iota(jnp.int32, (blk, 128), 1) < HD
    dk_acc[...] = jnp.zeros_like(dk_acc)
    dv_acc[...] = jnp.zeros_like(dv_acc)
    for i in range(slots // blk):
        first, n = i * blk, (i + 1) * blk
        bias = mask_bias(seq_ref, key_ref, first, blk)
        q2 = q_ref[first:n, :] * jnp.asarray(0.125, BF)
        do2 = do_ref[first:n, :]
        lse2 = lse_ref[first:n, :]
        prod = do2.astype(F32) * o_ref[first:n, :].astype(F32)
        k2 = k_ref[:n, :]
        v2 = v_ref[:n, :]
        dqs = []
        for h in range(2):
            qm = head_only(q2, lane, h)
            dom = head_only(do2, lane, h)
            delta = jnp.sum(head_only(prod, lane, h), axis=1, keepdims=True)
            p = jnp.exp(dot_t(qm, k2) + bias - lse2[:, h * HD : h * HD + 1])
            ds = (p * (dot_t(dom, v2) - delta)).astype(BF)
            dv_acc[:n, :] += dot_rows(p.astype(BF), dom)
            dk_acc[:n, :] += dot_rows(ds, qm)
            dqs.append(dot(ds, k2))
        dq = jnp.where(lane, dqs[0], dqs[1]) * 0.125
        dq_ref[first:n, :] = (dq * cos[first:n, :] - swap_halves(dq) * sin[first:n, :]).astype(BF)
    dk = dk_acc[...]
    dk_ref[...] = (dk * cos[...] - swap_halves(dk) * sin[...]).astype(BF)
    dv_ref[...] = dv_acc[...].astype(BF)


def attention_back(scal, half, qkv_all, o, do, lse, seq_col, key_row, cos, sin, deps):
    slots, width = o.shape
    pairs = width // 128
    count = pairs // 2
    third = lambda m: lambda i, s: (0, m * pairs + half * count + i)
    return call(
        "attention_back",
        13,
        functools.partial(attn_back_body, blk=256),
        scal,
        (count,),
        [(qkv_all, (slots, 128), third(m)) for m in range(3)]
        + [(a, (slots, 128), third(0)) for a in (o, do, lse)]
        + [(seq_col, (slots, 1), fixed(0, 0)), (key_row, (1, slots), fixed(0, 0))]
        + [(cos, (slots, 128), fixed(0, 0)), (sin, (slots, 128), fixed(0, 0))],
        [(sds((slots, width // 2)), (slots, 128), lambda i, s: (0, i))] * 3,
        deps,
        scratch=[pltpu.VMEM((slots, 128), F32)] * 2,
        limit=56,
    )


def tensor_body(s, *refs, n_pairs, op, mode):
    acc = None
    for p in range(n_pairs):
        term = op(refs[p][...], refs[n_pairs + p][...])
        acc = term if acc is None else acc + term
    rest = refs[2 * n_pairs :]
    if mode == "send":
        far, near = rest
        half = acc.shape[0] // 2
        low, high = acc[:half], acc[half:]
        far[...] = jnp.where(s[Y] == 0, high, low).astype(BF)
        near[...] = jnp.where(s[Y] == 0, low, high).astype(BF)
    else:
        got, out = rest
        out[...] = (acc + got[...].astype(F32)).astype(out.dtype)


def tensor_part(scal, mode, pairs, op, got, deps):
    slots = pairs[0][0].shape[0]
    quarter = slots // 4
    full = pairs[0][1].shape[1 if op is dot else 0]
    side = lambda at: lambda j, s: (j, at)
    tile = 512
    n_rows = 2 * quarter if mode == "send" else quarter
    row = {
        "send": lambda j, s: (1 - s[C], 0),
        "far": lambda j, s: (2 * s[C] + 1 - s[Y], 0),
        "near": lambda j, s: (2 * s[C] + s[Y], 0),
    }[mode]
    ins = [(a, (n_rows, a.shape[1]), row) for a, _, _ in pairs]
    for a, w, at in pairs:
        if op is dot:
            ins.append((w, (w.shape[0], tile), lambda j, s: (0, j)))
        else:
            ins.append((w, (tile, a.shape[1]), side(at)))
    col = lambda j, s: (0, j)
    if mode == "send":
        outs = [(sds((quarter, full)), (quarter, tile), col)] * 2
    else:
        ins.append((got, (quarter, tile), col))
        outs = [(sds((quarter, full), BF if mode == "far" else F32), (quarter, tile), col)]
    body = functools.partial(tensor_body, n_pairs=len(pairs), op=op, mode=mode)
    return call("tensor_" + mode, 5 if len(pairs) == 1 else 7, body, scal, (full // tile,), ins, outs, deps, limit=56)


def row_mean(v):
    return jnp.mean(v, axis=1, keepdims=True)


def own_quarter(g, s):
    return (quarter_of(s, 0), 0)


def back_of_norm(values, gain, upstream):
    inv = lax.rsqrt(row_mean(values * values) + 1e-05)
    gained = upstream * gain
    grad = jnp.sum(upstream * values * inv, axis=0, keepdims=True)
    return inv * gained - values * (inv * inv * inv) * row_mean(gained * values), grad


def joined(b0, from_x, from_y):
    return b0[...] + from_x[...].astype(F32) + from_y[...].astype(F32)


def norm2_back_body(s, b0, from_x, from_y, hres, live, gain, dm, da_out, back_out, grad_out):
    back, grad = back_of_norm(hres[...], gain[...].astype(F32), joined(b0, from_x, from_y))
    back_out[...] = back
    grad_out[...] = grad
    da_out[...] = (dm[...].astype(F32) + live[...] * back).astype(BF)


def norm2_back(scal, parts, hres, live, gain, dm, deps):
    rows, full = hres.shape
    whole = ((rows, full), fixed(0, 0))
    return call(
        "norm2_back", 7, norm2_back_body, scal, (1,),
        [(p, *whole) for p in parts]
        + [(hres, *whole), (live, (rows, 1), own_quarter), (gain, (1, full), fixed(0, 0)), (dm, *whole)],
        [(sds((rows, full)), *whole), (sds((rows, full), F32), *whole), (sds((1, full), F32), (1, full), fixed(0, 0))],
        deps,
    )


def feature_pieces(s, value, outs, hold):
    part = outs[0].shape[1]
    hold[...] = value.astype(BF)
    for k, out in enumerate(outs):
        out[...] = hold[:, pl.ds(pl.multiple_of(lax.bitwise_xor(s[T], k) * part, part), part)]


def norm1_back_body(s, near, back, x_own, gain, back_two, o0, o1, o2, o3, grad_out, hold):
    value, grad = back_of_norm(x_own[...].astype(F32), gain[...].astype(F32), near[...] + back[...].astype(F32))
    grad_out[...] = grad
    feature_pieces(s, value + back_two[...], (o0, o1, o2, o3), hold)


def norm1_back(scal, near, back, x_full, gain, back_two, deps):
    rows, full = near.shape
    whole = ((rows, full), fixed(0, 0))
    piece = (sds((rows, full // 4)), (rows, full // 4), fixed(0, 0))
    return call(
        "norm1_back", 6, norm1_back_body, scal, (1,),
        [(near, *whole), (back, *whole), (x_full, (rows, full), own_quarter), (gain, (1, full), fixed(0, 0)),
         (back_two, *whole)],
        [piece] * 4 + [(sds((1, full), F32), (1, full), fixed(0, 0))],
        deps,
        scratch=[pltpu.VMEM((rows, full), BF)],
        limit=56,
    )


def layer_body(s, b0, from_x, from_y, hres, live, o0, o1, o2, o3, hold):
    value = hres[...] + live[...] * joined(b0, from_x, from_y)
    feature_pieces(s, value, (o0, o1, o2, o3), hold)


def layer_rows(scal, parts, hres, live, deps):
    rows, full = hres.shape
    whole = ((rows, full), fixed(0, 0))
    piece = (sds((rows, full // 4)), (rows, full // 4), fixed(0, 0))
    return call(
        "layer_rows", 5, layer_body, scal, (1,),
        [(p, *whole) for p in parts]
        + [(hres, *whole), (live, (rows, 1), own_quarter)],
        [piece] * 4,
        deps,
        scratch=[pltpu.VMEM((rows, full), BF)],
    )


def place_body(s, *refs):
    out = refs[-1]
    rows = refs[0].shape[0]
    for k in range(4):
        at = pl.multiple_of(quarter_of(s, k) * rows, rows)
        value = refs[k][...]
        if len(refs) == 6:
            value = (value.astype(F32) + refs[4][pl.ds(at, rows), :].astype(F32)).astype(BF)
        out[pl.ds(at, rows), :] = value


def place_rows(scal, pieces, extra, deps):
    rows, cols = pieces[0].shape
    ins = [(p, (rows, cols), fixed(0, 0)) for p in pieces]
    if extra is not None:
        ins.append((extra, (4 * rows, cols), fixed(0, 0)))
    return call("place", 4, place_body, scal, (1,), ins, [(sds((4 * rows, cols)), (4 * rows, cols), fixed(0, 0))], deps)


def to_features(pieces):
    return [pieces[0], core_go(pieces[1]), y_go(pieces[2]), diag_go(pieces[3])]


def places():
    d, t = lax.axis_index("dp"), lax.axis_index("tensor")
    x, c, y = d % 2, t % 2, t // 2
    return x, c, y, {"tensor": t + 1 - 2 * c}, {"tensor": t + 2 - 4 * y}, {"dp": d + 1 - 2 * x}


def greet(*others):
    barrier = pltpu.get_barrier_semaphore()
    for other in others:
        pl.semaphore_signal(barrier, inc=1, device_id=other, device_id_type=pl.DeviceIdType.MESH)
    pl.semaphore_wait(barrier, len(others))


def remote(src, dst, send_sem, recv_sem, k, other):
    return pltpu.make_async_remote_copy(
        src_ref=src,
        dst_ref=dst,
        send_sem=send_sem.at[k],
        recv_sem=recv_sem.at[k],
        device_id=other,
        device_id_type=pl.DeviceIdType.MESH,
    )


def front_body(
    att, w_out, x_full, live, gain, dm0, dm0c, dmy, dmx, dmxc, wg, wu, wd,
    n2_out, hid_out, dga_out, dua_out, dm_out, down_out, hres_out,
    att_v, wo_v, xo_v, wg_v, wu_v, wd_v, n2_v, dm_v, snd, rcv, far_v, near_v, y_in, dyc, dxy, dxyc, hid_v, stage, sums,
    local, pieces_in, out_sem, whole_sem, sum_sem, send_sem, recv_sem,
):
    x, c, y, core, across_y, across_x = places()
    t = 2 * y + c
    rows, units, part = n2_v.shape[1], wg_v.shape[1], dmy.shape[1]

    def at(qc, qy):
        return pl.ds(pl.multiple_of((2 * qc + qy) * rows, rows), rows)

    def features(kc, ky):
        of = t + kc * (1 - 2 * c) + ky * (2 - 4 * y)
        return pl.ds(pl.multiple_of(of * part, part), part)

    dm_core = remote(dmy, dyc, send_sem, recv_sem, 3, core)
    dm_diag = remote(dmy, dxy, send_sem, recv_sem, 4, across_x)
    dm_on = remote(dxy, dxyc, send_sem, recv_sem, 5, core)
    half = pl.ds(pl.multiple_of(x * units, units), units)
    first = [
        pltpu.make_async_copy(att, att_v, local.at[0]),
        pltpu.make_async_copy(w_out, wo_v, local.at[1]),
        pltpu.make_async_copy(x_full.at[at(c, y), :], xo_v, local.at[2]),
    ]
    weights = [
        pltpu.make_async_copy(wg.at[:, half], wg_v, local.at[3]),
        pltpu.make_async_copy(wu.at[:, half], wu_v, local.at[4]),
        pltpu.make_async_copy(wd.at[half, :], wd_v, local.at[5]),
    ]
    for load in first:
        load.start()
    greet(core, across_y, across_x)
    dm_core.start()
    dm_diag.start()
    for load in weights:
        load.start()
    own_dm, pair_dm = [], []
    for r in range(8):
        ky, kx, kc = (r // 2) % 2, r // 4, r % 2
        from_rows = at(c + kc * (1 - 2 * c), y + ky * (1 - 2 * y))
        sources = ((dmx, 0, 0), (dmxc, 1, 0)) if kx else ((dm0, 0, 0), (dm0c, 1, 0), (dmy, 0, 1))
        for n, (source, fc, fy) in enumerate(sources):
            copy = pltpu.make_async_copy(
                source.at[from_rows, :], dm_v.at[r, :, features(fc, fy)], pieces_in.at[3 * r + n]
            )
            copy.start()
            (pair_dm if kx else own_dm).append(copy)

    for load in first:
        load.wait()

    def product(qc, qy, emit):
        left = att_v[at(qc, qy), :]
        for n in range(0, wo_v.shape[1], 256):
            emit(slice(n, n + 256), dot(left, wo_v[:, n : n + 256]))

    to_core = [remote(snd.at[k], rcv.at[k], send_sem, recv_sem, k, core) for k in range(2)]
    to_y = remote(far_v, y_in, send_sem, recv_sem, 2, across_y)
    for k, qy in enumerate((1 - y, y)):

        def put(cols, acc, k=k):
            snd[k, :, cols] = acc.astype(BF)

        product(1 - c, qy, put)
        to_core[k].start()
    to_core[0].wait_recv()

    def put_far(cols, acc):
        far_v[:, cols] = (acc + rcv[0, :, cols].astype(F32)).astype(BF)

    product(c, 1 - y, put_far)
    to_y.start()
    to_core[1].wait_recv()

    def put_near(cols, acc):
        near_v[:, cols] = acc + rcv[1, :, cols].astype(F32)

    product(c, y, put_near)
    for copy in own_dm:
        copy.wait()
    dm_core.wait_recv()
    for r in range(4):
        dm_v[r, :, features(1, 1)] = dyc[at(c + (r % 2) * (1 - 2 * c), y + (r // 2) * (1 - 2 * y)), :]

    to_y.wait_recv()
    hres = xo_v[...].astype(F32) + live[at(c, y), :] * (near_v[...] + y_in[...].astype(F32))
    hres_out[...] = hres
    n2_v[0] = (hres * lax.rsqrt(row_mean(hres * hres) + 1e-05) * gain[...].astype(F32)).astype(BF)

    def block_to(r_from, r_to, other):
        return remote(n2_v.at[r_from], n2_v.at[r_to], send_sem, recv_sem, 5 + r_to, other)

    n_y, n_x, n_c = block_to(0, 2, across_y), block_to(0, 4, across_x), block_to(0, 1, core)
    n_c.start()

    @pl.when(c == 0)
    def _():
        n_x.start()

    @pl.when(c == 1)
    def _():
        n_y.start()

    dm_diag.wait_recv()
    dm_on.start()
    for load in weights:
        load.wait()

    outs = (dga_out, dua_out)

    def order(i):
        inner = ((i + 2) // 4) % 2
        return i * (1 - inner) + inner * (2 + (2 * (1 - c) - i + 10) % 4)

    def store(i, k):
        place = pl.ds(pl.multiple_of(order(i) * rows, rows), rows)
        return pltpu.make_async_copy(stage.at[i % 2, k], outs[k].at[place, :], out_sem.at[i, k])

    def store_whole(i, source, out, k):
        place = pl.ds(pl.multiple_of(order(i) * rows, rows), rows)
        return pltpu.make_async_copy(source.at[order(i)], out.at[place, :], whole_sem.at[i, k])

    @pl.loop(0, 8)
    def _(i):
        r = order(i)

        @pl.when((i == 2) & (c == 0))
        def _():
            n_x.wait_send()
            n_y.start()
            n_x.wait_recv()
            block_to(4, 6, across_y).start()
            block_to(4, 5, core).start()

        @pl.when((i == 2) & (c == 1))
        def _():
            n_y.wait_send()
            n_x.start()
            n_y.wait_recv()
            block_to(2, 6, across_x).start()
            block_to(2, 3, core).start()

        @pl.when(i == 2)
        def _():
            for copy in pair_dm:
                copy.wait()
            dm_on.wait_recv()
            for b in range(4, 8):
                here = at(c + (b % 2) * (1 - 2 * c), y + ((b // 2) % 2) * (1 - 2 * y))
                dm_v[b, :, features(0, 1)] = dxy[here, :]
                dm_v[b, :, features(1, 1)] = dxyc[here, :]

        @pl.when((i == 4) & (c == 0))
        def _():
            n_y.wait_recv()
            block_to(2, 3, core).start()

        @pl.when((i == 4) & (c == 1))
        def _():
            n_x.wait_recv()
            block_to(4, 5, core).start()

        @pl.when((i == 1) | (i == 3) | (i == 5) | (i == 7))
        def _():
            block_to(0, r, core).wait_recv()

        @pl.when(i == 6)
        def _():
            block_to(2, 6, across_x).wait_recv()
            block_to(6, 7, core).start()

        store_whole(i, n2_v, n2_out, 0).start()
        store_whole(i, dm_v, dm_out, 1).start()

        @pl.when(i >= 2)
        def _():
            for k in range(2):
                store(i - 2, k).wait()

        for col in range(0, units, 256):
            cols = slice(col, col + 256)
            n = n2_v[r]
            ga = dot(n, wg_v[:, cols])
            ua = dot(n, wu_v[:, cols])
            dhid = dot_t(dm_v[r], wd_v[cols, :])
            sig = jax.nn.sigmoid(ga)
            silu = ga * sig
            hid_v[r, :, cols] = (silu * ua).astype(BF)
            stage[i % 2, 0, :, cols] = (dhid * ua * (sig * (1.0 + ga * (1.0 - sig)))).astype(BF)
            stage[i % 2, 1, :, cols] = (dhid * silu).astype(BF)
        for k in range(2):
            store(i, k).start()
        store_whole(i, hid_v, hid_out, 2).start()

    lines, width = sums.shape[1], sums.shape[3]

    def sum_store(u):
        here = pl.ds(pl.multiple_of(u * 256, 256), 256)
        return pltpu.make_async_copy(sums.at[u % 2], down_out.at[:, here, :], sum_sem.at[u])

    @pl.loop(0, units // 256)
    def _(u):
        @pl.when(u >= 2)
        def _():
            sum_store(u - 2).wait()

        turned = hid_v[:, :, pl.ds(pl.multiple_of(u * 256, 256), 256)].reshape(8 * rows, 256).T
        for n in range(0, lines * width, 256):
            value = dot(turned, dm_v[:, :, n : n + 256].reshape(8 * rows, 256)).astype(BF)
            piece = min(width, 256)
            for m in range(0, 256, piece):
                at_n = (n + m) % width
                sums[u % 2, (n + m) // width, :, at_n : at_n + piece] = value[:, m : m + piece]
        sum_store(u).start()

    for u in range(units // 256 - 2, units // 256):
        sum_store(u).wait()
    for i in (6, 7):
        for k in range(2):
            store(i, k).wait()

    @pl.loop(0, 8)
    def _(i):
        store_whole(i, n2_v, n2_out, 0).wait()
        store_whole(i, dm_v, dm_out, 1).wait()
        store_whole(i, hid_v, hid_out, 2).wait()

    @pl.when(c == 0)
    def _():
        n_y.wait_send()

    @pl.when(c == 1)
    def _():
        n_x.wait_send()

    for copy in (*to_core, to_y, dm_core, dm_diag, dm_on, n_c):
        copy.wait_send()
    for r_from, r_to in ((2, 3), (4, 5), (2, 6), (6, 7)):
        block_to(r_from, r_to, core).wait_send()


def front(att, w_out, x_full, live, gain, dm_pieces, wg, wu, wd, lines):
    slots, width = att.shape
    full = w_out.shape[1]
    rows, units, part = slots // 4, wg.shape[1] // 2, full // 4
    any_spec = pl.BlockSpec(memory_space=pl.ANY)
    vmem = pl.BlockSpec(memory_space=pltpu.VMEM)
    block = lambda *lead: pltpu.VMEM((*lead, rows, full), BF)
    piece = pltpu.VMEM((slots, part), BF)
    return pl.pallas_call(
        front_body,
        in_specs=[any_spec] * 3 + [vmem] * 2 + [any_spec] * 8,
        out_specs=[any_spec] * 6 + [vmem],
        out_shape=[sds((8 * rows, full))] + [sds((8 * rows, units))] * 3
        + [sds((8 * rows, full)), sds((lines, units, full // lines)), sds((rows, full), F32)],
        scratch_shapes=[
            pltpu.VMEM((slots, width), BF),
            pltpu.VMEM((width, full), BF),
            block(),
            pltpu.VMEM((full, units), BF),
            pltpu.VMEM((full, units), BF),
            pltpu.VMEM((units, full), BF),
            block(8),
            block(8),
            block(2),
            block(2),
            block(),
            pltpu.VMEM((rows, full), F32),
            block(),
            piece,
            piece,
            piece,
            pltpu.VMEM((8, rows, units), BF),
            pltpu.VMEM((2, 2, rows, units), BF),
            pltpu.VMEM((2, lines, 256, full // lines), BF),
            pltpu.SemaphoreType.DMA((6,)),
            pltpu.SemaphoreType.DMA((24,)),
            pltpu.SemaphoreType.DMA((8, 2)),
            pltpu.SemaphoreType.DMA((8, 3)),
            pltpu.SemaphoreType.DMA((units // 256,)),
            pltpu.SemaphoreType.DMA((13,)),
            pltpu.SemaphoreType.DMA((13,)),
        ],
        compiler_params=pltpu.CompilerParams(vmem_limit_bytes=62 * MIB, collective_id=2, has_side_effects=True),
        cost_estimate=pl.CostEstimate(flops=int(80 * 1.1e9), bytes_accessed=int(80 * 3.6e6), transcendentals=0),
        name="front",
    )(att, w_out, x_full, live, gain, *dm_pieces, wg, wu, wd)


def dn2_body(
    dga, dua, hid, wg, wu, wd, hres, dm, live, gain, da_out, back_out, grad_out, m_own, m_x, m_y,
    lefts, ws, wd_v, snd, rcv, kept, sb, via, via2, fx, fy, da_own, da_got, local, send_sem, recv_sem, credit,
):
    x, c, y, core, across_y, across_x = places()
    units, rows = wd_v.shape[0], snd.shape[1]
    half = pl.ds(pl.multiple_of(x * units, units), units)
    side = [slice(0, units), slice(units, 2 * units)]
    loads = [pltpu.make_async_copy(w.at[:, half], ws.at[:, side[p]], local.at[p]) for p, w in enumerate((wg, wu))]
    for kc in (1, 0):
        for p, left in enumerate((dga, dua)):
            loads.append(pltpu.make_async_copy(left.at[:, kc], lefts.at[kc, :, :, side[p]], local.at[2 + 2 * kc + p]))
    loads.append(pltpu.make_async_copy(hres, back_out, local.at[6]))
    loads.append(pltpu.make_async_copy(dm.at[pl.ds(0, rows), :], da_own, local.at[7]))
    loads.append(pltpu.make_async_copy(wd.at[half, :], wd_v, local.at[8]))
    hid_loads = [pltpu.make_async_copy(hid.at[:, kc], lefts.at[kc, :, :, side[0]], local.at[9 + kc]) for kc in range(2)]
    for load in loads:
        load.start()
    greet(core, across_y, across_x)
    for load in loads[:4]:
        load.wait()

    def tiles(kc, m, emit):
        for n in range(0, ws.shape[0], 256):
            emit(slice(n, n + 256), dot_t(lefts[kc, m], ws[n : n + 256, :]))

    def mlp_tiles(kc, m, emit):
        for n in range(0, wd_v.shape[1], 256):
            emit(slice(n, n + 256), dot(lefts[kc, m, :, :units], wd_v[:, n : n + 256]))

    def to_core(m, base):
        return remote(snd.at[m], rcv.at[m], send_sem, recv_sem, base + m, core)

    def send(m, make, base):
        def emit(cols, acc):
            snd[m, :, cols] = acc.astype(BF)

        make(1, m, emit)
        to_core(m, base).start()

    def keep(k, make, base):
        to_core(k, base).wait_recv()

        def emit(cols, acc):
            kept[k, :, cols] = acc + rcv[k, :, cols].astype(F32)

        make(0, k, emit)

    def diagonal_copy(dst, k, other):
        return remote(sb.at[0], dst, send_sem, recv_sem, k, other)

    def send_diagonal(dst, k):
        sb[0] = kept[3].astype(BF)

        @pl.when(c == 0)
        def _():
            diagonal_copy(dst, k, across_x).start()

        @pl.when(c == 1)
        def _():
            diagonal_copy(dst, k, across_y).start()

    @pl.loop(0, 4)
    def _(m):
        send(3 - m, tiles, 0)

    for load in loads[4:]:
        load.wait()
    go_x = remote(sb.at[1], fx, send_sem, recv_sem, 5, across_x)
    go_y = remote(sb.at[2], fy, send_sem, recv_sem, 6, across_y)

    @pl.loop(0, 4)
    def _(i):
        keep(3 - i, tiles, 0)

        @pl.when(i == 0)
        def _():
            send_diagonal(via, 4)

        @pl.when((i == 1) & (c == 0))
        def _():
            sb[1] = kept[2].astype(BF)
            go_x.start()

        @pl.when((i == 2) & (c == 1))
        def _():
            sb[2] = kept[1].astype(BF)
            go_y.start()

    pl.semaphore_signal(credit, inc=1, device_id=core, device_id_type=pl.DeviceIdType.MESH)
    for load in hid_loads:
        load.start()
    cf = c.astype(F32)
    diagonal_copy(via, 4, across_x).wait_recv()

    @pl.when(c == 1)
    def _():
        sb[1] = (kept[2] + via[...].astype(F32)).astype(BF)
        go_x.start()

    @pl.when(c == 0)
    def _():
        sb[2] = (kept[1] + via[...].astype(F32)).astype(BF)
        go_y.start()

    @pl.loop(0, 4)
    def _(m):
        to_core(m, 0).wait_send()

    pl.semaphore_wait(credit, 1)
    for load in hid_loads:
        load.wait()

    @pl.loop(0, 4)
    def _(m):
        send(3 - m, mlp_tiles, 10)

    go_x.wait_recv()
    go_y.wait_recv()
    dn2 = kept[0] + fx[...].astype(F32) + fy[...].astype(F32)
    back, grad = back_of_norm(back_out[...], gain[...].astype(F32), dn2)
    back_out[...] = back
    grad_out[...] = grad

    def at(qc, qy):
        return pl.ds(pl.multiple_of((2 * qc + qy) * rows, rows), rows)

    da_own[...] = (da_own[...].astype(F32) + live[at(c, y), :] * back).astype(BF)
    to_y = remote(da_own, da_got.at[1], send_sem, recv_sem, 8, across_y)
    to_c = remote(da_own, da_got.at[0], send_sem, recv_sem, 7, core)
    on = remote(da_got.at[1], da_got.at[2], send_sem, recv_sem, 9, core)
    to_y.start()
    to_c.start()
    da_out[at(c, y), :] = da_own[...]

    diagonal_copy(via, 4, across_x).wait_send()

    @pl.loop(0, 4)
    def _(i):
        keep(3 - i, mlp_tiles, 10)

        @pl.when(i == 0)
        def _():
            send_diagonal(via2, 14)

    for copy in (go_x, go_y):
        copy.wait_send()
    diagonal_copy(via2, 14, across_x).wait_recv()
    sb[1] = (kept[2] + cf * via2[...].astype(F32)).astype(BF)
    sb[2] = (kept[1] + (1.0 - cf) * via2[...].astype(F32)).astype(BF)
    stores = [
        pltpu.make_async_copy(source, out, local.at[11 + k])
        for k, (source, out) in enumerate(((kept.at[0], m_own), (sb.at[1], m_x), (sb.at[2], m_y)))
    ]
    for store in stores:
        store.start()
    to_c.wait_recv()
    da_out[at(1 - c, y), :] = da_got[0]
    to_y.wait_recv()
    on.start()
    da_out[at(c, 1 - y), :] = da_got[1]
    on.wait_recv()
    da_out[at(1 - c, 1 - y), :] = da_got[2]
    for store in stores:
        store.wait()

    @pl.loop(0, 4)
    def _(m):
        to_core(m, 10).wait_send()

    diagonal_copy(via2, 14, across_x).wait_send()
    for copy in (to_y, to_c, on):
        copy.wait_send()


def dn2_sum(dga, dua, hid, wg, wu, wd, hres, dm, live, gain, deps):
    tokens, units = dga.shape
    full = wg.shape[0]
    rows = tokens // 8
    slots = 4 * rows
    n_dep = len(deps)
    any_spec = pl.BlockSpec(memory_space=pl.ANY)
    vmem = pl.BlockSpec(memory_space=pltpu.VMEM)

    def body(*refs):
        dn2_body(*refs[:10], *refs[10 + n_dep :])

    block = lambda *lead: pltpu.VMEM((*lead, rows, full), BF)
    lefts = [v.reshape(4, 2, rows, units) for v in (dga, dua, hid)]
    return pl.pallas_call(
        body,
        in_specs=[any_spec] * 8 + [vmem] * 2 + [any_spec] * n_dep,
        out_specs=[vmem] * 3 + [any_spec] * 3,
        out_shape=[sds((slots, full)), sds((rows, full), F32), sds((1, full), F32), sds((rows, full), F32)]
        + [sds((rows, full))] * 2,
        scratch_shapes=[
            pltpu.VMEM((2, 4, rows, 2 * units), BF),
            pltpu.VMEM((full, 2 * units), BF),
            pltpu.VMEM((units, full), BF),
            block(4),
            block(4),
            pltpu.VMEM((4, rows, full), F32),
            block(3),
            block(),
            block(),
            block(),
            block(),
            block(),
            block(3),
            pltpu.SemaphoreType.DMA((14,)),
            pltpu.SemaphoreType.DMA((15,)),
            pltpu.SemaphoreType.DMA((15,)),
            pltpu.SemaphoreType.REGULAR,
        ],
        compiler_params=pltpu.CompilerParams(vmem_limit_bytes=62 * MIB, collective_id=1, has_side_effects=True),
        cost_estimate=pl.CostEstimate(flops=int(95 * 1.1e9), bytes_accessed=int(95 * 3.6e6), transcendentals=0),
        name="dn2_sum",
    )(*lefts, wg, wu, wd, hres, dm, live, gain, *deps)


def grad_body(s, a, b, *refs):
    out = refs[-1]
    a_t = a[...].T
    for col in range(0, b.shape[1], 256):
        out[0, :, col : col + 256] = dot(a_t, b[:, col : col + 256]).astype(BF)


def grad_by_rows(scal, a, b, lines, slot, slots, into, deps):
    tokens, m = a.shape
    n = b.shape[1]
    tile = min(256, m // lines)
    per = m // lines // tile
    ins = [(a, (tokens, tile), lambda j, s: (0, j)), (b, b.shape, fixed(0, 0))]
    if into is not None:
        ins.append((into, None, None))
    out = (sds((lines, m // lines, slots * n)), (1, tile, n), lambda j, s: (j // per, j % per, slot))
    aliases = None if into is None else {2: 0}
    return call("grad", 14, grad_body, scal, (m // tile,), ins, [out], deps, aliases=aliases, limit=56)


def line_sum(parts):
    n_dp = lax.axis_size("dp")
    groups = [[2 * z + x for z in range(n_dp // 2)] for x in range(2)]
    return lax.psum_scatter(parts, "dp", scatter_dimension=0, axis_index_groups=groups, tiled=False)


def pair_grad_body(s, a, *refs, n_b, keep):
    a_t = a[...].T
    out = refs[-1]
    width = refs[0].shape[1]
    for k in range(n_b):
        for col in range(0, width, 256):
            value = dot(a_t, refs[k][:, col : col + 256])
            at = k * width + col
            if keep:
                value = value + refs[n_b][0, :, at : at + 256].astype(F32)
            out[0, :, at : at + 256] = value.astype(BF)
    if n_b * width < out.shape[2]:
        out[0, :, n_b * width :] = refs[n_b + 1][0]


def pair_grad(scal, a, bs, lines, got, deps, extra=None):
    rows = a.shape[1] // (2 * lines)
    keep = got is not None
    member = (lambda s: s[X]) if keep else (lambda s: 1 - s[X])
    ins = [(a, (a.shape[0], rows), lambda j, s: (0, 2 * j + member(s)))]
    ins += [(b, b.shape, fixed(0, 0)) for b in bs]
    shard = lambda j, s: (j, 0, 0)
    total = bs[0].shape[1] * len(bs)
    for more in (got, extra):
        if more is not None:
            ins.append((more, (1, rows, more.shape[2]), shard))
    if extra is not None:
        total += extra.shape[2]
    outs = [(sds((lines, rows, total)), (1, rows, total), shard)]
    body = functools.partial(pair_grad_body, n_b=len(bs), keep=keep)
    name = "pair_grad_keep" if keep else "pair_grad_send"
    return call(name, 4 + total // 512, body, scal, (lines,), ins, outs, deps, limit=56)


def flip_body(s, total, out):
    out[...] = total[...].astype(F32).T


def flip(scal, total, first, width, deps):
    rows = total.shape[0]
    part = math.gcd(first, width)
    at = first // part
    return call(
        "flip", 3, flip_body, scal, (width // part,), [(total, (rows, part), lambda g, s: (0, at + g))],
        [(sds((width, rows), F32), (part, rows), lambda g, s: (g, 0))], deps,
    )


def halves_body(s, first, last, *outs):
    part = outs[0].shape[1] // 2
    for k, out in enumerate(outs):
        cols = slice(k * part, (k + 1) * part)
        out[:, :part] = first[:, cols].astype(F32)
        out[:, part:] = last[:, cols].astype(F32)


def head_halves(scal, first, last, part, deps):
    rows = first.shape[0]
    out = (sds((rows, 2 * part), F32), (rows, 2 * part), fixed(0, 0))
    return call(
        "head_halves", 3, halves_body, scal, (1,), [(v, v.shape, fixed(0, 0)) for v in (first, last)], [out] * 3, deps
    )


def pick(s, value, axis, other):
    half = value.shape[axis] // 2
    low, high = (value[:half], value[half:]) if axis == 0 else (value[:, :half], value[:, half:])
    return jnp.where(s[X] == (1 if other else 0), low, high)


def pair_send_body(s, total, out, *, axis):
    out[...] = pick(s, total[...], axis, True)


def pair_send(scal, total, axis, deps):
    shape = tuple(n // 2 if k == axis else n for k, n in enumerate(total.shape))
    body = functools.partial(pair_send_body, axis=axis)
    return call("pair_send", 3, body, scal, (1,), [(total, total.shape, fixed(0, 0))], [(sds(shape), shape, fixed(0, 0))], deps)


def hold_body(s, value, out):
    out[...] = value[...]


def hold(scal, value, deps):
    whole = (value.shape, fixed(0, 0))
    return call("hold", 2, hold_body, scal, (1,), [(value, *whole)], [(sds(value.shape), *whole)], deps)


def pair_join_body(s, total, got, *outs, axis):
    mine = pl.program_id(0) == s[X]
    width = got.shape[1] // len(outs)
    own = pick(s, total[...], axis, False)
    for k, out in enumerate(outs):
        cols = slice(k * width, (k + 1) * width)
        out[...] = jnp.where(mine, own[:, cols], got[:, cols]).astype(F32)


def pair_join(scal, total, got, axis, n_out, deps):
    rows, cols = got.shape
    cols //= n_out
    shape = (rows, 2 * cols) if axis == 0 else (2 * rows, cols)
    place = (lambda g, s: (0, g)) if axis == 0 else (lambda g, s: (g, 0))
    body = functools.partial(pair_join_body, axis=axis)
    return call(
        "pair_join", 4, body, scal, (2,),
        [(total, total.shape, fixed(0, 0)), (got, got.shape, fixed(0, 0))],
        [(sds(shape, F32), (rows, cols), place)] * n_out,
        deps,
    )


def gains_body(one, two, out, have, got, send_sem, recv_sem, *, lines):
    x, c, y, core, across_y, across_x = places()
    z = lax.axis_index("dp") // 2
    along = [{"dp": 2 * ((z + s) % lines) + x} for s in range(1, lines)]
    greet(core, across_y, across_x, *along)
    have[0, 0:1, :] = one[...]
    have[0, 1:2, :] = two[...]
    copies = []
    for k, other in enumerate((core, across_y, across_x)):
        copy = remote(have.at[k], got.at[k], send_sem, recv_sem, k, other)
        copy.start()
        copy.wait_recv()
        have[k + 1] = have[k] + got[k]
        copies.append(copy)
    last = [remote(have.at[3], got.at[3 + s], send_sem, recv_sem, 3 + s, other) for s, other in enumerate(along)]
    for copy in last:
        copy.start()
    total = have[3]
    for s, copy in enumerate(last):
        copy.wait_recv()
        total = total + got[3 + s]
    out[...] = total
    for copy in copies + last:
        copy.wait_send()


def gains_sum(one, two, lines, deps):
    full = one.shape[1]
    vmem = pl.BlockSpec(memory_space=pltpu.VMEM)
    n = 2 + lines

    def body(one, two, *refs):
        gains_body(one, two, *refs[len(deps) :], lines=lines)

    return pl.pallas_call(
        body,
        in_specs=[vmem] * 2 + [pl.BlockSpec(memory_space=pl.ANY)] * len(deps),
        out_specs=vmem,
        out_shape=sds((2, full), F32),
        scratch_shapes=[
            pltpu.VMEM((4, 2, full), F32),
            pltpu.VMEM((n, 2, full), F32),
            pltpu.SemaphoreType.DMA((n,)),
            pltpu.SemaphoreType.DMA((n,)),
        ],
        compiler_params=pltpu.CompilerParams(vmem_limit_bytes=24 * MIB, collective_id=3, has_side_effects=True),
        cost_estimate=pl.CostEstimate(flops=int(12 * 1.1e9), bytes_accessed=int(12 * 3.6e6), transcendentals=0),
        name="gains",
    )(one, two, *deps)


def layout(tile_len, tile_offset):
    tiles = tile_len.shape[0]
    within = jnp.arange(TILE, dtype=jnp.int32)[None, :]
    live = within < tile_len[:, None]
    position = (tile_offset[:, None] * TILE + within).astype(F32)
    seq = jnp.cumsum((tile_offset == 0).astype(jnp.int32))
    seq = jnp.broadcast_to(seq[:, None], (tiles, TILE))
    key = jnp.where(live, seq, -1)
    slots = tiles * TILE
    return live.astype(F32).reshape(slots, 1), position.reshape(slots), seq.reshape(slots, 1), key.reshape(1, slots)


def rope_tables(position):
    frequency = jnp.power(130000.0, -2.0 * jnp.arange(HD // 2, dtype=F32) / HD)
    angles = position[:, None] * frequency[None, :]
    c, s = jnp.cos(angles), jnp.sin(angles)
    return jnp.concatenate([c, c, c, c], axis=1), jnp.concatenate([-s, s, -s, s], axis=1)


def gather_tensor(own):
    far = y_go(own)
    return [own, core_go(own), far, core_go(far)]


def shards(
    hidden_in,
    norm1_gain,
    w_query,
    w_key,
    w_value,
    w_out,
    norm2_gain,
    w_gate,
    w_up,
    w_down,
    tile_len,
    tile_offset,
    cotangent,
):
    n_dp = lax.axis_size("dp")
    lines = n_dp // 2
    d, t = lax.axis_index("dp").astype(jnp.int32), lax.axis_index("tensor").astype(jnp.int32)
    zz, xx = d // 2, d % 2
    yy, cc = t // 2, t % 2
    scal = jnp.stack([t, cc, yy, xx, zz])
    full = w_query.shape[0]
    rows_dp = full // n_dp
    gain_one, gain_two = norm1_gain[None, :], norm2_gain[None, :]
    live, position, seq_col, key_row = layout(tile_len, tile_offset)
    cos, sin = rope_tables(position)

    pieces = gather_tensor(hidden_in)
    dm_own = (cotangent.astype(F32) * live).astype(BF)
    dm_x = x_go(dm_own)
    dm_pieces = [dm_own, core_go(dm_own), y_go(dm_own), dm_x, core_go(dm_x)]

    x_full, n1, qkv_all = qkv(scal, pieces, gain_one, w_query, w_key, w_value, cos, sin, ())
    attended, lse = attention(scal, qkv_all, seq_col, key_row, ())
    n2, hid, dga, dua, dm, down_parts, hres = front(
        attended, w_out, x_full, live, gain_two, dm_pieces, w_gate, w_up, w_down, lines
    )

    narrow = rows_dp % 128 == 0
    down_sum = line_sum(down_parts)
    gate_up = grad_by_rows(scal, n2, dga, lines, 0, 2, None, ())
    gate_up = grad_by_rows(scal, n2, dua, lines, 1, 2, gate_up, ())
    ups_sum = line_sum(gate_up)
    da, back_two, grad_two, m_own, m_x, m_y = dn2_sum(
        dga, dua, hid, w_gate, w_up, w_down, hres, dm, live, gain_two, (gate_up,)
    )
    dob = dob_rows(scal, da, w_out, ())
    back_args = (qkv_all, attended, dob, lse, seq_col, key_row, cos, sin)
    if narrow:
        out_sent = pair_grad(scal, da, [attended], lines, None, (dob,))
        out_got = x_go(out_sent)
        back_a = attention_back(scal, 0, *back_args, (out_sent,))
        sent_a = pair_grad(scal, n1, back_a, lines, None, ())
        got_a = x_go(sent_a)
        m_x = hold(scal, m_x, (sent_a,))
        back_b = attention_back(scal, 1, *back_args, (m_x,))
        sent_b = pair_grad(scal, n1, back_b, lines, None, ())
        got_b = x_go(sent_b)
        out_parts = pair_grad(scal, da, [attended], lines, out_got, (sent_b,))
        last = out_parts
    else:
        back_a = attention_back(scal, 0, *back_args, ())
        back_b = attention_back(scal, 1, *back_args, ())
        last = back_b[0]
    if narrow:
        first_parts = pair_grad(scal, n1, back_a, lines, got_a, (last,), out_parts)
        last = first_parts
    layer_parts = layer_rows(scal, (m_own, x_go(m_x), y_go(m_y)), hres, live, (last,))
    layer_pieces = to_features(layer_parts)
    last = layer_parts[0]
    dn1_pairs = [(v, w, k) for k, back in enumerate((back_a, back_b)) for v, w in zip(back, (w_query, w_key, w_value))]
    send_far, send_near = tensor_part(scal, "send", dn1_pairs, dot_t, None, (last,))
    far = tensor_part(scal, "far", dn1_pairs, dot_t, core_go(send_far), ())
    down_send = pair_send(scal, down_sum, 1, (far,))
    ups_send = pair_send(scal, ups_sum, 0, (down_send,))
    layer_out = place_rows(scal, layer_pieces, None, (ups_send,))
    near = tensor_part(scal, "near", dn1_pairs, dot_t, core_go(send_near), (layer_out,))
    last = near
    if narrow:
        last_parts = pair_grad(scal, n1, back_b, lines, got_b, (near,))
        last = last_parts
    else:
        *first, out_parts = wide_pair_grads(xx, [(n1, v) for v in back_a] + [(da, attended)], lines)
        first_parts = jnp.concatenate(first + [out_parts], axis=2)
        last_parts = jnp.concatenate(wide_pair_grads(xx, [(n1, v) for v in back_b], lines), axis=2)
    first_sum, last_sum = line_sum(first_parts), line_sum(last_parts)
    *in_parts, grad_one = norm1_back(scal, near, y_go(far), x_full, gain_one, back_two, (last,))
    in_pieces = to_features(in_parts)
    part = back_a[0].shape[1]
    out_grad = flip(scal, first_sum, 3 * part, 2 * part, (grad_one,))
    down_grad = pair_join(scal, down_sum, x_go(down_send), 1, 1, (out_grad,))
    all_gains = gains_sum(grad_one, grad_two, lines, (down_grad,))
    gains = lax.dynamic_slice_in_dim(all_gains, d * rows_dp, rows_dp, 1)
    gate_grad, up_grad = pair_join(scal, ups_sum, x_go(ups_send), 0, 2, (all_gains,))
    input_grad = place_rows(scal, in_pieces, cotangent, (gate_grad,))
    query_grad, key_grad, value_grad = head_halves(scal, first_sum, last_sum, part, (input_grad,))
    return (
        layer_out,
        input_grad,
        gains[0],
        query_grad,
        key_grad,
        value_grad,
        out_grad,
        gains[1],
        gate_grad,
        up_grad,
        down_grad,
    )


def dob_body(s, da, w, out):
    out[...] = dot_t(da[...], w[...]).astype(BF)


def dob_rows(scal, da, w_out, deps):
    slots, full = da.shape
    width = w_out.shape[0]
    blk = 512
    return call(
        "dob", 6, dob_body, scal, (slots // blk,),
        [(da, (blk, full), lambda i, s: (i, 0)), (w_out, (width, full), fixed(0, 0))],
        [(sds((slots, width)), (blk, width), lambda i, s: (i, 0))],
        deps,
    )


def wide_pair_grads(xx, pairs, lines):
    sums = []
    for a, b in pairs:
        parts = dot_rows(a, b).astype(BF)
        parts = parts.reshape(lines, 2, parts.shape[0] // (2 * lines), parts.shape[1])
        got = x_go(lax.dynamic_index_in_dim(parts, 1 - xx, 1, keepdims=False))
        keep = lax.dynamic_index_in_dim(parts, xx, 1, keepdims=False)
        sums.append((keep.astype(F32) + got.astype(F32)).astype(BF))
    return sums


def solution(mesh):
    in_specs = (
        P("dp", "tensor"),
        P(),
        P(None, "tensor"),
        P(None, "tensor"),
        P(None, "tensor"),
        P("tensor", None),
        P(),
        P(None, "tensor"),
        P(None, "tensor"),
        P("tensor", None),
        P("dp"),
        P("dp"),
        P("dp", "tensor"),
    )
    out_specs = (
        P("dp", "tensor"),
        P("dp", "tensor"),
        P("dp"),
        P("dp", "tensor"),
        P("dp", "tensor"),
        P("dp", "tensor"),
        P("tensor", "dp"),
        P("dp"),
        P("dp", "tensor"),
        P("dp", "tensor"),
        P("tensor", "dp"),
    )
    return jax.shard_map(shards, mesh=mesh, in_specs=in_specs, out_specs=out_specs, check_vma=False)
```
